256 devices in a mesh: az: 32 (over z_hi, y, x), rad: 8 (over z_lo, core).
Axes of the slice: x: 4, y: 4, z: 8 (z_hi: 2, z_lo: 4; z = z_hi * 4 + z_lo), core: 2. Of those that a mesh axis runs over, the one named last changes fastest.
Arguments:
- density: float32 [2, 2048, 16384], P(None, 'rad', 'az'), may hold values from 0.5 to 2
- mom_r: float32 [2, 2048, 16384], P(None, 'rad', 'az'), may hold values from -1 to 1
- mom_phi: float32 [2, 2048, 16384], P(None, 'rad', 'az'), may hold values from 0.5 to 1.5
- potential_kernel: bfloat16 [64, 2048, 2048], P('az', 'rad'), may hold values from -2 to 2
- force_kernel: bfloat16 [64, 2048, 2048], P('az', 'rad'), may hold values from -2 to 2
Outputs:
- new_density: float32 [2, 2048, 16384], P(None, 'rad', 'az')
- new_mom_r: float32 [2, 2048, 16384], P(None, 'rad', 'az')
- new_mom_phi: float32 [2, 2048, 16384], P(None, 'rad', 'az')
- potential: float32 [2048, 16384], P('rad', 'az')
The draws below stay inside these ranges and needn't reach their ends.
All inputs are finite; a program needn't handle non-finite values.
Results may differ from the reference program's by a relative error of at most 0.0015.
The reference program's roundings to bfloat16 on the way count: a program that leaves them out, or rounds other values in their place, can miss the bound.
Values may be sent and summed in bfloat16 or wider, within the bound.
A program may use at most 128 MiB of HBM per device.

```python
import math
import jax
import jax.numpy as jnp
from jax import lax

NR = 2048
NAZ = 16384
MODES = 64
LAYERS = 2


def kernel_law(key):
    mode_index = jnp.arange(MODES)
    amplitude = jnp.where(mode_index == 0, 1.0 / LAYERS, math.sqrt(NAZ / (MODES * LAYERS))).astype(jnp.float32)
    entries = jax.random.truncated_normal(key, -4.0, 4.0, (MODES, NR, NR), jnp.float32)
    return (entries * amplitude[:, None, None] / math.sqrt(NR)).astype(jnp.bfloat16)


def draw_potential_kernel(key, part):
    return kernel_law(jax.random.fold_in(key, 11))


def draw_force_kernel(key, part):
    return kernel_law(jax.random.fold_in(key, 23))


def steps_of(rng, shape, shards, low, high):
    level = 1.0
    for axis_at, blocks in shards:
        heights = jax.random.uniform(jax.random.fold_in(jax.random.fold_in(rng, 6), axis_at), (blocks,), jnp.float32, low / len(shards), high / len(shards))
        level = level * jnp.repeat(jnp.exp(heights), shape[axis_at] // blocks).reshape((-1,) + (1,) * (len(shape) - 1 - axis_at))
    return level


def centred(rng, shape, width, most, pieces=(), kind=jnp.bfloat16):
    values = jax.random.normal(rng, shape, jnp.float32) * width
    if len(pieces) > 0:
        values = steps_of(rng, shape, pieces, -0.22, 0.18) * values
    return jnp.clip(values, min=-most, max=most).astype(kind)


def setup_inputs(seed: int = 0) -> dict:
    splits = jax.random.split(jax.random.key(seed), 6)
    density = jnp.clip(0.5 + 1.5 * jax.random.uniform(splits[0], (LAYERS, NR, NAZ), jnp.float32) ** steps_of(splits[0], (LAYERS, NR, NAZ), ((1, 8), (2, 32)), -0.2, 0.2), 0.5, 2.0)
    mom_r = centred(splits[1], (LAYERS, NR, NAZ), 0.2, 1.0, ((1, 8), (2, 32)), jnp.float32)
    mom_phi = jnp.clip(0.5 + 1.0 * jax.random.uniform(splits[2], (LAYERS, NR, NAZ), jnp.float32) ** steps_of(splits[2], (LAYERS, NR, NAZ), ((1, 8), (2, 32)), -0.2, 0.2), 0.5, 1.5)
    potential_kernel = draw_potential_kernel(jax.random.fold_in(splits[5], 71), 0)
    force_kernel = draw_force_kernel(jax.random.fold_in(splits[5], 71), 0)
    return dict(density=density, mom_r=mom_r, mom_phi=mom_phi, potential_kernel=potential_kernel, force_kernel=force_kernel)


aspect_sq = 0.0025

def mode_table(azimuth):
    mode_index = jnp.arange(MODES).astype(jnp.float32)
    angles = azimuth[:, None] * mode_index[None, :]
    basis = jnp.stack([jnp.cos(angles), jnp.sin(angles)], axis=-1).reshape(azimuth.shape[0], 2 * MODES)
    slope = jnp.stack([-mode_index * jnp.sin(angles), mode_index * jnp.cos(angles)], axis=-1).reshape(azimuth.shape[0], 2 * MODES)
    return (basis, slope)

def radial_flux(lower_side, upper_side, sound):

    def physical(fields):
        velocity = fields[1] / fields[0]
        flux = jnp.stack([fields[1], fields[1] * velocity + sound * fields[0], fields[2] * velocity])
        return (flux, velocity)
    flux_lower, vel_lower = physical(lower_side)
    flux_upper, vel_upper = physical(upper_side)
    wave_speed = jnp.maximum(jnp.abs(vel_lower), jnp.abs(vel_upper)) + jnp.sqrt(sound)
    return 0.5 * (flux_lower + flux_upper) - 0.5 * wave_speed * (upper_side - lower_side)

def azimuth_flux(lower_side, upper_side, sound):

    def physical(fields):
        velocity = fields[2] / fields[0]
        flux = jnp.stack([fields[2], fields[1] * velocity, fields[2] * velocity + sound * fields[0]])
        return (flux, velocity)
    flux_lower, vel_lower = physical(lower_side)
    flux_upper, vel_upper = physical(upper_side)
    wave_speed = jnp.maximum(jnp.abs(vel_lower), jnp.abs(vel_upper)) + jnp.sqrt(sound)
    return 0.5 * (flux_lower + flux_upper) - 0.5 * wave_speed * (upper_side - lower_side)

def tendency(fields, radial_ext, azimuth_ext, face_radius, grav_radial, grav_azimuth, cell_step):
    inner_radius = face_radius[:-1]
    outer_radius = face_radius[1:]
    mid_radius = 0.5 * (inner_radius + outer_radius)
    cell_area = 0.5 * (outer_radius * outer_radius - inner_radius * inner_radius)
    sound_face = (aspect_sq / face_radius)[:, None]
    sound_mid = (aspect_sq / mid_radius)[:, None]
    flux_rad = radial_flux(radial_ext[:, :, :-1], radial_ext[:, :, 1:], sound_face)
    flux_azi = azimuth_flux(azimuth_ext[..., :-1], azimuth_ext[..., 1:], sound_mid)
    weighted = flux_rad * face_radius[:, None]
    divergence = (weighted[:, :, 1:] - weighted[:, :, :-1]) / cell_area[:, None]
    divergence = divergence + (flux_azi[..., 1:] - flux_azi[..., :-1]) / (mid_radius[:, None] * cell_step)
    surface_now = fields[0]
    radial_mom = fields[1]
    spin_mom = fields[2]
    centre = mid_radius[:, None]
    source_rad = (spin_mom * spin_mom / surface_now + sound_mid * surface_now) / centre
    source_rad = source_rad + surface_now * (grav_radial / cell_step - 1.0 / (centre * centre))
    source_azi = -radial_mom * spin_mom / (surface_now * centre) + surface_now * (grav_azimuth / cell_step)
    source = jnp.stack([jnp.zeros_like(surface_now), source_rad, source_azi])
    return fields + 0.1 * cell_step * (source - divergence)

def reference(density, mom_r, mom_phi, potential_kernel, force_kernel):
    highest = lax.Precision.HIGHEST
    cell_step = 2.0 * math.pi / NAZ
    azimuth = (jnp.arange(NAZ).astype(jnp.float32) + 0.5) * cell_step
    basis, slope = mode_table(azimuth)
    surface = lax.optimization_barrier(jnp.sum(density, axis=0))
    density_modes = jnp.dot(surface, basis, precision=highest) / NAZ
    rounded = lax.optimization_barrier(density_modes.astype(jnp.bfloat16))
    mode_pairs = rounded.astype(jnp.float32).reshape(NR, MODES, 2)
    pot_modes = jnp.einsum('krs,skc->rkc', potential_kernel.astype(jnp.float32), mode_pairs, precision=highest).reshape(NR, 2 * MODES)
    force_modes = jnp.einsum('krs,skc->rkc', force_kernel.astype(jnp.float32), mode_pairs, precision=highest).reshape(NR, 2 * MODES)
    potential = jnp.dot(pot_modes, basis.T, precision=highest)
    grav_radial = jnp.dot(force_modes, basis.T, precision=highest)
    face_radius = jnp.exp(jnp.arange(NR + 1).astype(jnp.float32) * cell_step)
    mid_radius = 0.5 * (face_radius[:-1] + face_radius[1:])
    grav_azimuth = -jnp.dot(pot_modes, slope.T, precision=highest) / mid_radius[:, None]
    fields = jnp.stack([density, mom_r, mom_phi])
    updated = []
    for layer_index in range(LAYERS):
        column = fields[:, layer_index:layer_index + 1]
        radial_ext = jnp.concatenate([column[:, :, :1], column, column[:, :, -1:]], axis=2)
        azimuth_ext = jnp.concatenate([column[..., -1:], column, column[..., :1]], axis=3)
        updated.append(tendency(column, radial_ext, azimuth_ext, face_radius, grav_radial, grav_azimuth, cell_step))
    result = jnp.concatenate(updated, axis=1)
    return (result[0], result[1], result[2], potential)
```

```python
import math

import jax
import jax.numpy as jnp
import ml_dtypes
import numpy as np
from jax import lax
from jax.experimental import pallas as pl
from jax.experimental.pallas import tpu as pltpu
from jax.sharding import PartitionSpec as P

NR = 2048
NAZ = 16384
MODES = 64
AZ = 32
RAD = 8
HALF = 16
LAYERS = 2
ROWS = NR // RAD
CELLS = NAZ // AZ
STEP = 2.0 * math.pi / NAZ
ASPECT_SQ = 0.0025
MESH = pl.DeviceIdType.MESH
F32 = jnp.float32
BF16 = jnp.bfloat16
NT = (((1,), (1,)), ((), ()))
NN = (((1,), (0,)), ((), ()))


def split(table):
    high = table.astype(ml_dtypes.bfloat16)
    low = (table - high.astype(np.float64)).astype(ml_dtypes.bfloat16)
    return (high, low)


def mode_tables():
    p, h, j = np.meshgrid(np.arange(16), np.arange(2), np.arange(4), indexing="ij")
    column = (4 * (16 * h + p) + j).reshape(-1)
    mode = (column // 2).astype(np.float64)
    odd = (column % 2).astype(bool)
    azimuth = (np.arange(NAZ) + 0.5) * STEP
    angle = mode[:, None] * azimuth[None, :]
    cos, sin = np.cos(angle), np.sin(angle)
    basis = np.where(odd[:, None], sin, cos)
    slope = np.where(odd[:, None], mode[:, None] * cos, -mode[:, None] * sin)
    tables = np.stack([*split(basis), *split(slope)])
    return np.ascontiguousarray(tables.reshape(4, 128, AZ, CELLS).transpose(2, 0, 1, 3))


def row_table():
    face = np.exp(np.arange(NR + 1) * STEP)
    inner, outer = face[:-1], face[1:]
    mid = 0.5 * (inner + outer)
    area = 0.5 * (outer * outer - inner * inner)
    table = np.zeros((NR, 128), np.float32)
    columns = [
        ASPECT_SQ / outer,
        np.sqrt(ASPECT_SQ / outer),
        0.05 * STEP * outer / area,
        0.05 * STEP * inner / area,
        ASPECT_SQ / mid,
        np.sqrt(ASPECT_SQ / mid),
        0.05 / mid,
        0.1 * STEP / mid,
        0.1 * STEP * (ASPECT_SQ / mid / mid - 1.0 / (mid * mid)),
        -0.1 / mid,
        ASPECT_SQ / inner,
        np.sqrt(ASPECT_SQ / inner),
    ]
    for k, values in enumerate(columns):
        table[:, k] = values
    return table


def face_flux(low, high, sound, sound_root, pressed):
    rho_l, mr_l, mp_l, v_l = low
    rho_h, mr_h, mp_h, v_h = high
    speed = jnp.maximum(jnp.abs(v_l), jnp.abs(v_h)) + sound_root
    a, b = v_l + speed, v_h - speed
    flux = [rho_l * a + rho_h * b, mr_l * a + mr_h * b, mp_l * a + mp_h * b]
    flux[pressed] = flux[pressed] + sound * (rho_l + rho_h)
    return flux


def exchange(
    density,
    mom_r,
    mom_phi,
    pot_kernel,
    force_kernel,
    tables,
    rows,
    coef,
    part,
    fluid,
    tab,
    kern,
    rtab,
    surf,
    chunks,
    arrived,
    halfsum,
    gathered,
    az_out,
    az_in,
    rad_out,
    rad_in,
    az_cols,
    carry,
    load_sem,
    send_sem,
    recv_sem,
    edge_send,
    edge_recv,
):
    az = lax.axis_index("az")
    rad = lax.axis_index("rad")
    z_hi = az // HALF
    p = az % HALF
    q = z_hi * RAD + rad
    az_next, az_prev = (az + 1) % AZ, (az + AZ - 1) % AZ
    rad_next, rad_prev = (rad + 1) % RAD, (rad + RAD - 1) % RAD
    plane = [(z_hi * HALF + (p + k) % HALF, rad) for k in range(1, HALF)]
    column = [
        (((q + k) % 16) // RAD * HALF + p, ((q + k) % 16) % RAD) for k in range(1, 16)
    ]
    partner = ((az + HALF) % AZ, rad)

    inside = pl.ds(8, ROWS)
    loads = [
        pltpu.make_async_copy(density, fluid.at[0, :, inside, :], load_sem.at[0]),
        pltpu.make_async_copy(tables.at[az], tab, load_sem.at[1]),
        pltpu.make_async_copy(mom_r, fluid.at[1, :, inside, :], load_sem.at[2]),
        pltpu.make_async_copy(mom_phi, fluid.at[2, :, inside, :], load_sem.at[3]),
        pltpu.make_async_copy(rows.at[pl.ds(rad * ROWS, ROWS), :], rtab, load_sem.at[4]),
        pltpu.make_async_copy(pot_kernel, kern.at[0], load_sem.at[5]),
        pltpu.make_async_copy(force_kernel, kern.at[1], load_sem.at[6]),
    ]
    for load in loads:
        load.start()

    barrier = pltpu.get_barrier_semaphore()
    greeted = plane + column + [(az_next, rad), (az_prev, rad)]
    for device in greeted:
        pl.semaphore_signal(barrier, inc=1, device_id=device, device_id_type=MESH)

    loads[0].wait()

    @pl.loop(0, ROWS // 32)
    def _(block):
        at = pl.multiple_of(block * 32, 32)
        value = fluid[0, 0, pl.ds(8 + at, 32), :] + fluid[0, 1, pl.ds(8 + at, 32), :]
        high = value.astype(BF16)
        surf[0, pl.ds(at, 32), :] = high
        surf[1, pl.ds(at, 32), :] = (value - high.astype(F32)).astype(BF16)

    loads[1].wait()
    share = lax.dot_general(tab[0], surf[0], NT, preferred_element_type=F32)
    share += lax.dot_general(tab[0], surf[1], NT, preferred_element_type=F32)
    share += lax.dot_general(tab[1], surf[0], NT, preferred_element_type=F32)
    chunks[...] = share.reshape(HALF, 8, ROWS)

    pl.semaphore_wait(barrier, len(greeted))

    sends = []
    for k, (az_to, rad_to) in enumerate(plane):
        copy = pltpu.make_async_remote_copy(
            src_ref=chunks.at[(p + k + 1) % HALF],
            dst_ref=arrived.at[k],
            send_sem=send_sem.at[0],
            recv_sem=recv_sem.at[0],
            device_id=(az_to, rad_to),
            device_id_type=MESH,
        )
        copy.start()

    loads[2].wait()
    loads[3].wait()
    row_id = lax.broadcasted_iota(jnp.int32, (8, 128), 0)
    lane_id = lax.broadcasted_iota(jnp.int32, (8, 128), 1)
    for side, (lanes, lane) in enumerate(((pl.ds(0, 128), 0), (pl.ds(CELLS - 128, 128), 127))):
        total = jnp.zeros((8, ROWS), F32)
        for f in range(6):
            pick = jnp.where((row_id == f) & (lane_id == lane), 1.0, 0.0).astype(BF16)
            block = fluid[f // 2, f % 2, inside, lanes].astype(BF16)
            total += lax.dot_general(pick, block, NT, preferred_element_type=F32)
        az_out[side] = total
    for f in range(6):
        rad_out[0, f : f + 1, :] = fluid[f // 2, f % 2, 8:9, :]
        rad_out[1, f : f + 1, :] = fluid[f // 2, f % 2, 8 + ROWS - 1 : 8 + ROWS, :]
    rad_out[0, 6:8, :] = jnp.zeros((2, CELLS), F32)
    rad_out[1, 6:8, :] = jnp.zeros((2, CELLS), F32)
    edges = []
    for n, (src, dst, device) in enumerate(
        (
            (az_out.at[0], az_in.at[1], (az_prev, rad)),
            (az_out.at[1], az_in.at[0], (az_next, rad)),
            (rad_out.at[0], rad_in.at[1], (az, rad_prev)),
            (rad_out.at[1], rad_in.at[0], (az, rad_next)),
        )
    ):
        copy = pltpu.make_async_remote_copy(
            src_ref=src,
            dst_ref=dst,
            send_sem=edge_send.at[n],
            recv_sem=edge_recv.at[n],
            device_id=device,
            device_id_type=MESH,
        )
        copy.start()
        edges.append(copy)

    fifteen = arrived.at[pl.ds(0, 15)]
    pltpu.make_async_copy(fifteen, fifteen, recv_sem.at[0]).wait()
    total = chunks[p]
    for k in range(15):
        total = total + arrived[k]
    for h in range(2):
        halfsum[h, 0:4, :] = total[4 * h : 4 * h + 4, 0:128]
        halfsum[h, 4:8, :] = total[4 * h : 4 * h + 4, 128:256]
    gathered[q] = halfsum[z_hi]
    for k, (az_to, rad_to) in enumerate(column):
        copy = pltpu.make_async_remote_copy(
            src_ref=halfsum.at[az_to // HALF],
            dst_ref=gathered.at[q],
            send_sem=send_sem.at[1],
            recv_sem=recv_sem.at[1],
            device_id=(az_to, rad_to),
            device_id_type=MESH,
        )
        copy.start()

    loads[4].wait()
    for edge in edges:
        edge.wait()
    az_cols[0] = az_in[0].T
    az_cols[1] = az_in[1].T
    for f in range(6):
        field, layer = f // 2, f % 2
        inner = jnp.where(rad == 0, rad_out[0, f : f + 1, :], rad_in[0, f : f + 1, :])
        outer = jnp.where(rad == RAD - 1, rad_out[1, f : f + 1, :], rad_in[1, f : f + 1, :])
        fluid[field, layer, 0:8, :] = jnp.broadcast_to(inner, (8, CELLS))
        fluid[field, layer, 8 + ROWS : 16 + ROWS, :] = jnp.broadcast_to(outer, (8, CELLS))

    wide_row = lax.broadcasted_iota(jnp.int32, (8, CELLS), 0)
    wide_lane = lax.broadcasted_iota(jnp.int32, (8, CELLS), 1)

    def state(layer, at):
        rho = fluid[0, layer, pl.ds(at, 8), :]
        mr = fluid[1, layer, pl.ds(at, 8), :]
        mp = fluid[2, layer, pl.ds(at, 8), :]
        return (rho, mr, mp)

    def up(now, later):
        return pltpu.roll(jnp.where(wide_row == 0, later, now), 7, 0)

    def radial(now, later, sound, sound_root):
        inv_now, inv_later = 1.0 / now[0], 1.0 / later[0]
        low = (*now, now[1] * inv_now)
        late = (*later, later[1] * inv_later)
        high = [up(a, b) for a, b in zip(low, late)]
        return face_flux(low, high, sound, sound_root, 1), inv_now

    for layer in range(LAYERS):
        flux, _ = radial(
            state(layer, 0), state(layer, 8), rtab[0:1, 10:11], rtab[0:1, 11:12]
        )
        for c in range(3):
            carry[c, layer] = flux[c]

    def update(block):
        at = pl.multiple_of(block * 8, 8)
        here = pl.ds(at, 8)

        def factor(k):
            return jnp.broadcast_to(rtab[here, k : k + 1], (8, CELLS))

        for layer in range(LAYERS):
            now, later = state(layer, at + 8), state(layer, at + 16)
            flux, inv = radial(now, later, factor(0), factor(1))
            rho, mr, mp = now
            vp = mp * inv
            cells = (rho, mr, mp, vp)
            left = []
            for c in range(4):
                left.append(pltpu.roll(cells[c], 1, 1))
            lo_cols = [az_cols[0, here, 2 * c + layer : 2 * c + layer + 1] for c in range(3)]
            hi_cols = [az_cols[1, here, 2 * c + layer : 2 * c + layer + 1] for c in range(3)]
            lo_cols.append(lo_cols[2] / lo_cols[0])
            hi_cols.append(hi_cols[2] / hi_cols[0])
            left = [jnp.where(wide_lane == 0, jnp.broadcast_to(a, (8, CELLS)), b) for a, b in zip(lo_cols, left)]
            aflux = face_flux(left, cells, factor(4), factor(5), 2)
            last = [cell[:, CELLS - 1 :] for cell in cells]
            lflux = face_flux(last, hi_cols, rtab[here, 4:5], rtab[here, 5:6], 2)
            new = []
            for c in range(3):
                below = pltpu.roll(jnp.where(wide_row == 7, carry[c, layer], flux[c]), 1, 0)
                above = pltpu.roll(aflux[c], CELLS - 1, 1)
                above = jnp.where(wide_lane == CELLS - 1, jnp.broadcast_to(lflux[c], (8, CELLS)), above)
                change = factor(2) * flux[c] - factor(3) * below + factor(6) * (above - aflux[c])
                carry[c, layer] = flux[c]
                new.append(now[c] - change)
            turn = factor(7) * vp
            new[1] = new[1] + (turn * mp + factor(8) * rho)
            new[2] = new[2] - turn * mr
            for c in range(3):
                part[c, layer, here, :] = new[c]

    def update_range(start, stop):
        @pl.loop(start, stop)
        def _(block):
            update(block)

    update_range(0, 12)

    loads[5].wait()
    loads[6].wait()
    fifteen = gathered.at[pl.ds(0, 15)]
    pltpu.make_async_copy(fifteen, fifteen, recv_sem.at[1]).wait()
    pieces = []
    for r in range(RAD):
        both = (gathered[r] + gathered[RAD + r]) * (1.0 / NAZ)
        pieces += [both[0:4], both[4:8]]
    modes = jnp.concatenate(pieces, axis=1)
    modes = jnp.concatenate([modes, jnp.zeros_like(modes)], axis=0).astype(BF16)
    for which in range(2):
        for m in range(2):
            product = lax.dot_general(modes, kern[which, m], NT, preferred_element_type=F32)
            coef[az, 4 * which + 2 * m : 4 * which + 2 * m + 2, :] = product[2 * m : 2 * m + 2, :]

    cross = pltpu.make_async_remote_copy(
        src_ref=coef.at[az],
        dst_ref=coef.at[az],
        send_sem=send_sem.at[2],
        recv_sem=recv_sem.at[2],
        device_id=partner,
        device_id_type=MESH,
    )
    cross.start()
    for az_to, rad_to in plane:
        pltpu.make_async_remote_copy(
            src_ref=coef.at[az],
            dst_ref=coef.at[az],
            send_sem=send_sem.at[3],
            recv_sem=recv_sem.at[3],
            device_id=(az_to, rad_to),
            device_id_type=MESH,
        ).start()
    update_range(12, 20)
    cross.wait_recv()
    for az_to, rad_to in plane:
        pltpu.make_async_remote_copy(
            src_ref=coef.at[partner[0]],
            dst_ref=coef.at[partner[0]],
            send_sem=send_sem.at[4],
            recv_sem=recv_sem.at[4],
            device_id=(az_to, rad_to),
            device_id_type=MESH,
        ).start()
    update_range(20, 32)

    fifteen = coef.at[pl.ds(0, 15)]
    pltpu.make_async_copy(fifteen, fifteen, recv_sem.at[3]).wait()
    pltpu.make_async_copy(fifteen, fifteen, recv_sem.at[4]).wait()
    cross.wait_send()
    for n in (0, 3, 4):
        pltpu.make_async_copy(fifteen, fifteen, send_sem.at[n]).wait()
    fifteen = gathered.at[pl.ds(0, 15)]
    pltpu.make_async_copy(fifteen, fifteen, send_sem.at[1]).wait()


def finish(coef, part, fluid, tab, rtab, out_density, out_r, out_phi, out_pot, pot_buf, mom_buf, sem):
    first = pltpu.make_async_copy(part.at[0], out_density, sem.at[0])
    first.start()
    row_id = lax.broadcasted_iota(jnp.int32, (8, ROWS), 0)
    pots, forces = [], []
    for n in range(HALF):
        a, b = coef[n], coef[HALF + n]
        pots.append(jnp.where(row_id < 4, a, pltpu.roll(b, 4, 0)))
        forces.append(jnp.where(row_id < 4, pltpu.roll(a, 4, 0), b))

    def sides(tiles):
        value = jnp.concatenate(tiles, axis=0).T
        high = value.astype(BF16)
        return high, (value - high.astype(F32)).astype(BF16)

    def product(sides, table, rows):
        high, low = sides[0][rows], sides[1][rows]
        out = lax.dot_general(high, tab[table], NN, preferred_element_type=F32)
        out += lax.dot_general(low, tab[table], NN, preferred_element_type=F32)
        return out + lax.dot_general(high, tab[table + 1], NN, preferred_element_type=F32)

    pot, force = sides(pots), sides(forces)
    block = 64
    copies = []
    for n in range(ROWS // block):
        here = slice(n * block, (n + 1) * block)
        pot_buf[here, :] = product(pot, 0, here)
        radial = 0.1 * product(force, 0, here)
        azimuthal = product(pot, 2, here) * rtab[here, 9:10]
        inside = slice(8 + n * block, 8 + (n + 1) * block)
        for layer in range(LAYERS):
            rho = fluid[0, layer, inside, :]
            mom_buf[0, layer, here, :] = part[1, layer, here, :] + rho * radial
            mom_buf[1, layer, here, :] = part[2, layer, here, :] + rho * azimuthal
        for k, (src, dst) in enumerate(
            (
                (pot_buf.at[pl.ds(n * block, block), :], out_pot.at[pl.ds(n * block, block), :]),
                (mom_buf.at[0, :, pl.ds(n * block, block), :], out_r.at[:, pl.ds(n * block, block), :]),
                (mom_buf.at[1, :, pl.ds(n * block, block), :], out_phi.at[:, pl.ds(n * block, block), :]),
            )
        ):
            copy = pltpu.make_async_copy(src, dst, sem.at[1 + 3 * n + k])
            copy.start()
            copies.append(copy)
    first.wait()
    for copy in copies:
        copy.wait()


def local(density, mom_r, mom_phi, potential_kernel, force_kernel):
    tables = jnp.asarray(mode_tables())
    rows = jnp.asarray(row_table())
    operands = (density, mom_r, mom_phi, potential_kernel, force_kernel, tables, rows)
    hbm = pl.BlockSpec(memory_space=pltpu.HBM)
    vmem = pl.BlockSpec(memory_space=pltpu.VMEM)
    dma = pltpu.SemaphoreType.DMA
    shared = (
        ((AZ, 8, ROWS), F32),
        ((3, LAYERS, ROWS, CELLS), F32),
        ((3, LAYERS, ROWS + 16, CELLS), F32),
        ((4, 128, CELLS), BF16),
        ((ROWS, 128), F32),
    )
    coef, part, fluid, tab, rtab = pl.pallas_call(
        exchange_call,
        out_shape=[pltpu.VMEM(shape, dtype) for shape, dtype in shared],
        in_specs=[hbm] * 7,
        out_specs=[vmem] * 5,
        scratch_shapes=[
            pltpu.VMEM((2, 2, ROWS, NR), BF16),
            pltpu.VMEM((2, ROWS, CELLS), BF16),
            pltpu.VMEM((HALF, 8, ROWS), F32),
            pltpu.VMEM((15, 8, ROWS), F32),
            pltpu.VMEM((2, 8, 128), F32),
            pltpu.VMEM((16, 8, 128), F32),
            pltpu.VMEM((2, 8, ROWS), F32),
            pltpu.VMEM((2, 8, ROWS), F32),
            pltpu.VMEM((2, 8, CELLS), F32),
            pltpu.VMEM((2, 8, CELLS), F32),
            pltpu.VMEM((2, ROWS, 8), F32),
            pltpu.VMEM((3, LAYERS, 8, CELLS), F32),
            dma((7,)),
            dma((5,)),
            dma((5,)),
            dma((4,)),
            dma((4,)),
        ],
        compiler_params=pltpu.CompilerParams(
            collective_id=0, has_side_effects=True, vmem_limit_bytes=32 * 2**20
        ),
        name="exchange",
    )(*(pltpu.with_memory_space_constraint(a, pltpu.HBM) for a in operands))
    fluid_shape = jax.ShapeDtypeStruct((LAYERS, ROWS, CELLS), F32)
    return pl.pallas_call(
        finish,
        out_shape=[fluid_shape, fluid_shape, fluid_shape, jax.ShapeDtypeStruct((ROWS, CELLS), F32)],
        in_specs=[vmem] * 5,
        out_specs=[hbm] * 4,
        scratch_shapes=[
            pltpu.VMEM((ROWS, CELLS), F32),
            pltpu.VMEM((2, LAYERS, ROWS, CELLS), F32),
            dma((1 + 3 * 4,)),
        ],
        compiler_params=pltpu.CompilerParams(vmem_limit_bytes=32 * 2**20),
        name="finish",
    )(coef, part, fluid, tab, rtab)


def exchange_call(d, r, f, pk, fk, tables, rows, coef, part, fluid, tab, rtab, kern, *rest):
    exchange(d, r, f, pk, fk, tables, rows, coef, part, fluid, tab, kern, rtab, *rest)


def solution(mesh):
    fluid = P(None, "rad", "az")
    kernel = P("az", "rad", None)
    return jax.shard_map(
        local,
        mesh=mesh,
        in_specs=(fluid, fluid, fluid, kernel, kernel),
        out_specs=(fluid, fluid, fluid, P("rad", "az")),
        check_vma=False,
    )
```

```python
import math

import jax
import jax.numpy as jnp
import ml_dtypes
import numpy as np
from jax import lax
from jax.experimental import pallas as pl
from jax.experimental.pallas import tpu as pltpu
from jax.sharding import PartitionSpec as P

NR = 2048
NAZ = 16384
MODES = 64
AZ = 32
RAD = 8
HALF = 16
LAYERS = 2
ROWS = NR // RAD
CELLS = NAZ // AZ
STEP = 2.0 * math.pi / NAZ
ASPECT_SQ = 0.0025
MESH = pl.DeviceIdType.MESH
F32 = jnp.float32
BF16 = jnp.bfloat16
NT = (((1,), (1,)), ((), ()))
NN = (((1,), (0,)), ((), ()))


def split(table):
    high = table.astype(ml_dtypes.bfloat16)
    low = (table - high.astype(np.float64)).astype(ml_dtypes.bfloat16)
    return (high, low)


def mode_tables():
    p, h, j = np.meshgrid(np.arange(16), np.arange(2), np.arange(4), indexing="ij")
    column = (4 * (16 * h + p) + j).reshape(-1)
    mode = (column // 2).astype(np.float64)
    odd = (column % 2).astype(bool)
    azimuth = (np.arange(NAZ) + 0.5) * STEP
    angle = mode[:, None] * azimuth[None, :]
    cos, sin = np.cos(angle), np.sin(angle)
    basis = np.where(odd[:, None], sin, cos)
    slope = np.where(odd[:, None], mode[:, None] * cos, -mode[:, None] * sin)
    tables = np.stack([*split(basis), *split(slope)])
    return np.ascontiguousarray(tables.reshape(4, 128, AZ, CELLS).transpose(2, 0, 1, 3))


def row_tables():
    face = np.exp(np.arange(NR + 1) * STEP)
    inner, outer = face[:-1], face[1:]
    mid = 0.5 * (inner + outer)
    area = 0.5 * (outer * outer - inner * inner)
    table = np.zeros((NR, 128), np.float32)
    columns = [
        ASPECT_SQ / outer,
        np.sqrt(ASPECT_SQ / outer),
        0.05 * STEP * outer / area,
        0.05 * STEP * inner / area,
        ASPECT_SQ / mid,
        np.sqrt(ASPECT_SQ / mid),
        0.05 / mid,
        0.1 * STEP / mid,
        0.1 * STEP * (ASPECT_SQ / mid / mid - 1.0 / (mid * mid)),
        -0.1 / mid,
        ASPECT_SQ / inner,
        np.sqrt(ASPECT_SQ / inner),
    ]
    for k, values in enumerate(columns):
        table[:, k] = values
    across = np.zeros((8, NR), np.float32)
    for k, n in enumerate((4, 5, 6)):
        across[k] = columns[n]
    return (table, across)


def face_flux(low, high, sound, sound_root, pressed):
    rho_l, mr_l, mp_l, v_l = low
    rho_h, mr_h, mp_h, v_h = high
    speed = jnp.maximum(jnp.abs(v_l), jnp.abs(v_h)) + sound_root
    a, b = v_l + speed, v_h - speed
    flux = [rho_l * a + rho_h * b, mr_l * a + mr_h * b, mp_l * a + mp_h * b]
    flux[pressed] = flux[pressed] + sound * (rho_l + rho_h)
    return flux


def reciprocal(value):
    guess = pl.reciprocal(value, approx=True)
    return guess * (2.0 - value * guess)


def whole(ref, count):
    slots = ref.at[pl.ds(0, count)]
    return lambda sem: pltpu.make_async_copy(slots, slots, sem).wait()


def radial_flux(low, high, sound, sound_root):
    return face_flux(
        (*low, low[1] * reciprocal(low[0])),
        (*high, high[1] * reciprocal(high[0])),
        sound,
        sound_root,
        1,
    )


def azimuth_flux(low, high, sound, sound_root):
    return face_flux(
        (*low, low[2] * reciprocal(low[0])),
        (*high, high[2] * reciprocal(high[0])),
        sound,
        sound_root,
        2,
    )


def pairs_of(ref, at):
    value = ref[at]
    return [value[2 * c : 2 * c + 2] for c in range(3)]


def exchange(
    density,
    mom_r,
    mom_phi,
    pot_kernel,
    force_kernel,
    tables,
    rows,
    lanes,
    coef,
    part,
    fluid,
    tab,
    rtab,
    kern,
    ltab,
    surf,
    chunks,
    arrived,
    halfsum,
    gathered,
    az_out,
    az_in,
    az_swap,
    rad_out,
    rad_in,
    carry,
    load_sem,
    send_sem,
    recv_sem,
    column_sem,
    edge_send,
    edge_recv,
):
    az = lax.axis_index("az")
    rad = lax.axis_index("rad")
    z_hi = az // HALF
    p = az % HALF
    y, x = p // 4, p % 4
    z, core = z_hi * 4 + rad // 2, rad % 2
    q = z_hi * RAD + rad
    partner = ((az + HALF) % AZ, rad)

    far = [(2, 2), (1, 2), (2, 1), (3, 2), (2, 3), (1, 1), (3, 3), (1, 3), (3, 1), (2, 0), (0, 2), (0, 1), (1, 0), (0, 3), (3, 0)]
    plane = [(y + dy) % 4 * 4 + (x + dx) % 4 for dy, dx in far]
    column = []
    for dz, dc in [(4, 0), (4, 1), (3, 0), (5, 0), (3, 1), (5, 1), (2, 0), (6, 0), (2, 1), (6, 1), (1, 0), (7, 0), (1, 1), (7, 1), (0, 1)]:
        there = (z + dz) % 8
        column.append((there // 4, there % 4 * 2 + (core + dc) % 2))

    barrier = pltpu.get_barrier_semaphore()
    for to in plane:
        pl.semaphore_signal(barrier, inc=1, device_id=(z_hi * HALF + to, rad), device_id_type=MESH)
    for half, to in column:
        pl.semaphore_signal(barrier, inc=1, device_id=(half * HALF + p, to), device_id_type=MESH)

    inside = pl.ds(8, ROWS)
    loads = [
        pltpu.make_async_copy(density, fluid.at[0, :, inside, :], load_sem.at[0]),
        pltpu.make_async_copy(tables.at[az], tab, load_sem.at[1]),
        pltpu.make_async_copy(mom_r, fluid.at[1, :, inside, :], load_sem.at[2]),
        pltpu.make_async_copy(mom_phi, fluid.at[2, :, inside, :], load_sem.at[3]),
        pltpu.make_async_copy(rows.at[pl.ds(rad * ROWS, ROWS), :], rtab, load_sem.at[4]),
        pltpu.make_async_copy(lanes.at[:, pl.ds(rad * ROWS, ROWS)], ltab, load_sem.at[5]),
        pltpu.make_async_copy(pot_kernel, kern.at[0], load_sem.at[6]),
        pltpu.make_async_copy(force_kernel, kern.at[1], load_sem.at[7]),
    ]
    for load in loads:
        load.start()

    loads[0].wait()

    @pl.loop(0, ROWS // 32)
    def _(block):
        at = pl.multiple_of(block * 32, 32)
        value = fluid[0, 0, pl.ds(8 + at, 32), :] + fluid[0, 1, pl.ds(8 + at, 32), :]
        high = value.astype(BF16)
        surf[0, pl.ds(at, 32), :] = high
        surf[1, pl.ds(at, 32), :] = (value - high.astype(F32)).astype(BF16)

    loads[1].wait()
    share = lax.dot_general(tab[0], surf[0], NT, preferred_element_type=F32)
    share += lax.dot_general(tab[0], surf[1], NT, preferred_element_type=F32)
    share += lax.dot_general(tab[1], surf[0], NT, preferred_element_type=F32)
    chunks[...] = share.reshape(HALF, 8, ROWS)

    pl.semaphore_wait(barrier, len(plane) + len(column))

    for k, to in enumerate(plane):
        pltpu.make_async_remote_copy(
            src_ref=chunks.at[to],
            dst_ref=arrived.at[k],
            send_sem=send_sem.at[0],
            recv_sem=recv_sem.at[0],
            device_id=(z_hi * HALF + to, rad),
            device_id_type=MESH,
        ).start()

    loads[2].wait()
    loads[3].wait()
    row_id = lax.broadcasted_iota(jnp.int32, (8, 256), 0)
    lane_id = lax.broadcasted_iota(jnp.int32, (8, 256), 1)
    for side, (at, lane) in enumerate(((0, 0), (CELLS - 128, 127))):
        total = jnp.zeros((8, ROWS), F32)
        for c in range(3):
            both = jnp.concatenate([fluid[c, n, inside, at : at + 128] for n in range(2)], axis=1)
            pick = jnp.where(lane_id == lane + 128 * (row_id - 2 * c), 1.0, 0.0)
            pick = jnp.where((row_id == 2 * c) | (row_id == 2 * c + 1), pick, 0.0).astype(BF16)
            high = both.astype(BF16)
            low = (both - high.astype(F32)).astype(BF16)
            total += lax.dot_general(pick, high, NT, preferred_element_type=F32)
            total += lax.dot_general(pick, low, NT, preferred_element_type=F32)
        az_out[side] = total
    rad_out[...] = jnp.zeros_like(rad_out)
    for f in range(6):
        rad_out[0, f : f + 1, :] = fluid[f // 2, f % 2, 8:9, :]
        rad_out[1, f : f + 1, :] = fluid[f // 2, f % 2, 8 + ROWS - 1 : 8 + ROWS, :]
    edges = []
    for n, (src, dst, device) in enumerate(
        (
            (az_out.at[0], az_in.at[1], (z_hi * HALF + (p + HALF - 1) % HALF, rad)),
            (az_out.at[1], az_in.at[0], (z_hi * HALF + (p + 1) % HALF, rad)),
            (rad_out.at[0], rad_in.at[1], (az, (rad + RAD - 1) % RAD)),
            (rad_out.at[1], rad_in.at[0], (az, (rad + 1) % RAD)),
        )
    ):
        copy = pltpu.make_async_remote_copy(
            src_ref=src,
            dst_ref=dst,
            send_sem=edge_send.at[n],
            recv_sem=edge_recv.at[n],
            device_id=device,
            device_id_type=MESH,
        )
        copy.start()
        edges.append(copy)

    loads[4].wait()
    for c in range(3):
        for layer in range(LAYERS):
            fluid[c, layer, 0:8, :] = jnp.broadcast_to(fluid[c, layer, 8:9, :], (8, CELLS))
            fluid[c, layer, 8 + ROWS : 16 + ROWS, :] = jnp.broadcast_to(
                fluid[c, layer, 7 + ROWS : 8 + ROWS, :], (8, CELLS)
            )
    for layer in range(LAYERS):
        edge = [fluid[c, layer, 0:8, :] for c in range(3)]
        flux = radial_flux(edge, edge, rtab[0:1, 10:11], rtab[0:1, 11:12])
        for c in range(3):
            carry[c, layer] = flux[c]

    size = 32

    @pl.loop(0, ROWS // size)
    def _(block):
        at = pl.multiple_of(block * size, size)
        here = pl.ds(at, size)

        def factor(k):
            return jnp.broadcast_to(rtab[here, k : k + 1], (size, CELLS))

        for layer in range(LAYERS):
            state = [fluid[c, layer, pl.ds(at + 8, size + 8), :] for c in range(3)]
            inv = reciprocal(state[0])
            state.append(state[1] * inv)
            low = [value[:size] for value in state]
            high = [pltpu.roll(value, size + 7, 0)[:size] for value in state]
            flux = face_flux(low, high, factor(0), factor(1), 1)
            rho, mr, mp = low[:3]
            vp = mp * inv[:size]
            cells = (rho, mr, mp, vp)
            left = [pltpu.roll(value, 1, 1) for value in cells]
            side = face_flux(left, cells, factor(4), factor(5), 2)
            new = []
            for c in range(3):
                below = pltpu.roll(jnp.concatenate([carry[c, layer], flux[c]], axis=0), 1, 0)[8:]
                above = pltpu.roll(side[c], CELLS - 1, 1)
                carry[c, layer] = flux[c][size - 8 :]
                new.append(
                    low[c]
                    - (factor(2) * flux[c] - factor(3) * below + factor(6) * (above - side[c]))
                )
            turn = factor(7) * vp
            new[1] = new[1] + (turn * mp + factor(8) * rho)
            new[2] = new[2] - turn * mr
            for c in range(3):
                part[c, layer, here, :] = new[c]

    whole(arrived, 15)(recv_sem.at[0])
    total = chunks[p]
    for k in range(15):
        total = total + arrived[k]
    for h in range(2):
        halfsum[h, 0:4, :] = total[4 * h : 4 * h + 4, 0:128]
        halfsum[h, 4:8, :] = total[4 * h : 4 * h + 4, 128:256]
    gathered[z_hi, rad] = halfsum[z_hi]
    for half, to in column:
        pltpu.make_async_remote_copy(
            src_ref=halfsum.at[half],
            dst_ref=gathered.at[z_hi, rad],
            send_sem=send_sem.at[1],
            recv_sem=column_sem.at[(rad - to + RAD) % RAD],
            device_id=(half * HALF + p, to),
            device_id_type=MESH,
        ).start()

    edges[2].wait()
    edges[3].wait()
    for side, (outermost, sign, weight, sound) in enumerate(
        ((rad == 0, 1.0, rtab[0:1, 3:4], 10), (rad == RAD - 1, -1.0, rtab[ROWS - 1 : ROWS, 2:3], 0))
    ):
        row = 0 if side == 0 else ROWS - 1
        sounds = (rtab[row : row + 1, sound : sound + 1], rtab[row : row + 1, sound + 1 : sound + 2])
        own = pairs_of(rad_out, side)
        beyond = [jnp.where(outermost, a, b) for a, b in zip(own, pairs_of(rad_in, side))]
        used = radial_flux(own, own, *sounds)
        right = radial_flux(beyond, own, *sounds) if side == 0 else radial_flux(own, beyond, *sounds)
        for c in range(3):
            delta = (sign * weight) * (right[c] - used[c])
            for layer in range(LAYERS):
                part[c, layer, row : row + 1, :] = part[c, layer, row : row + 1, :] + delta[layer : layer + 1]

    edges[0].wait()
    edges[1].wait()
    end = p // (HALF - 1)
    swap = pltpu.make_async_remote_copy(
        src_ref=az_in.at[end],
        dst_ref=az_swap,
        send_sem=edge_send.at[4],
        recv_sem=edge_recv.at[4],
        device_id=partner,
        device_id_type=MESH,
    )
    at_end = (p == 0) | (p == HALF - 1)

    @pl.when(at_end)
    def _():
        swap.start()

    loads[6].wait()
    loads[7].wait()
    products = [jnp.zeros((16, ROWS), F32) for _ in range(4)]
    for k in (0, 1, 7, 2, 6, 3, 5, 4):
        from_rad = (rad + k) % RAD
        pair = gathered.at[:, from_rad] if k else gathered.at[pl.ds(0, 1), from_rad]
        pltpu.make_async_copy(pair, pair, column_sem.at[k]).wait()
        both = (gathered[0, from_rad] + gathered[1, from_rad]) * (1.0 / NAZ)
        modes = jnp.concatenate([both[0:4], both[4:8]], axis=1)
        modes = jnp.concatenate([modes] * 4, axis=0).astype(BF16)
        at = pl.ds(pl.multiple_of(from_rad * ROWS, ROWS), ROWS)
        for n in range(4):
            products[n] += lax.dot_general(modes, kern[n // 2, n % 2, :, at], NT, preferred_element_type=F32)
    for n in range(4):
        m = n % 2
        coef[az, 2 * n : 2 * n + 2, :] = products[n][2 * m : 2 * m + 2]

    cross = pltpu.make_async_remote_copy(
        src_ref=coef.at[az],
        dst_ref=coef.at[az],
        send_sem=send_sem.at[2],
        recv_sem=recv_sem.at[1],
        device_id=partner,
        device_id_type=MESH,
    )
    cross.start()

    def to_plane(slot, n):
        for to in plane:
            pltpu.make_async_remote_copy(
                src_ref=coef.at[slot],
                dst_ref=coef.at[slot],
                send_sem=send_sem.at[1 + n],
                recv_sem=recv_sem.at[n],
                device_id=(z_hi * HALF + to, rad),
                device_id_type=MESH,
            ).start()

    to_plane(az, 2)

    @pl.when(at_end)
    def _():
        swap.wait()
        az_in[end] = az_swap[...]

    loads[5].wait()
    own_low, own_high = pairs_of(az_out, 0), pairs_of(az_out, 1)
    sounds = (ltab[0:1, :], ltab[1:2, :])
    used = azimuth_flux(own_high, own_low, *sounds)
    below = azimuth_flux(pairs_of(az_in, 0), own_low, *sounds)
    above = azimuth_flux(own_high, pairs_of(az_in, 1), *sounds)
    blank = jnp.zeros((2, ROWS), F32)
    weight = ltab[2:3, :]
    first = jnp.concatenate([weight * (a - b) for a, b in zip(below, used)] + [blank], axis=0)
    last = jnp.concatenate([weight * (b - a) for a, b in zip(above, used)] + [blank], axis=0)
    lane_id = lax.broadcasted_iota(jnp.int32, (ROWS, 128), 1)
    for at, lane, rim in ((0, 0, first.T), (CELLS - 128, 127, last.T)):
        for f in range(6):
            here = (f // 2, f % 2, slice(None), pl.ds(at, 128))
            delta = jnp.broadcast_to(rim[:, f : f + 1], (ROWS, 128))
            part[here] = part[here] + jnp.where(lane_id == lane, delta, 0.0)

    cross.wait_recv()
    to_plane(partner[0], 3)
    for n in (2, 3):
        whole(coef, 15)(recv_sem.at[n])
    cross.wait_send()
    for n in (0, 3, 4):
        whole(coef, 15)(send_sem.at[n])
    whole(coef.at[:, :, pl.ds(0, 128)], 15)(send_sem.at[1])


def finish(coef, part, fluid, tab, rtab, out_density, out_r, out_phi, out_pot, pot_buf, mom_buf, sem):
    first = pltpu.make_async_copy(part.at[0], out_density, sem.at[0])
    first.start()
    row_id = lax.broadcasted_iota(jnp.int32, (8, ROWS), 0)
    pots, forces = [], []
    for n in range(HALF):
        a, b = coef[n], coef[HALF + n]
        pots.append(jnp.where(row_id < 4, a, pltpu.roll(b, 4, 0)))
        forces.append(jnp.where(row_id < 4, pltpu.roll(a, 4, 0), b))

    def sides(tiles):
        value = jnp.concatenate(tiles, axis=0).T
        high = value.astype(BF16)
        return high, (value - high.astype(F32)).astype(BF16)

    def product(sides, table, rows):
        high, low = sides[0][rows], sides[1][rows]
        out = lax.dot_general(high, tab[table], NN, preferred_element_type=F32)
        out += lax.dot_general(low, tab[table], NN, preferred_element_type=F32)
        return out + lax.dot_general(high, tab[table + 1], NN, preferred_element_type=F32)

    pot, force = sides(pots), sides(forces)
    block = 64
    copies = []
    for n in range(ROWS // block):
        here = slice(n * block, (n + 1) * block)
        pot_buf[here, :] = product(pot, 0, here)
        radial = 0.1 * product(force, 0, here)
        azimuthal = product(pot, 2, here) * rtab[here, 9:10]
        inside = slice(8 + n * block, 8 + (n + 1) * block)
        for layer in range(LAYERS):
            rho = fluid[0, layer, inside, :]
            mom_buf[0, layer, here, :] = part[1, layer, here, :] + rho * radial
            mom_buf[1, layer, here, :] = part[2, layer, here, :] + rho * azimuthal
        for k, (src, dst) in enumerate(
            (
                (pot_buf.at[pl.ds(n * block, block), :], out_pot.at[pl.ds(n * block, block), :]),
                (mom_buf.at[0, :, pl.ds(n * block, block), :], out_r.at[:, pl.ds(n * block, block), :]),
                (mom_buf.at[1, :, pl.ds(n * block, block), :], out_phi.at[:, pl.ds(n * block, block), :]),
            )
        ):
            copy = pltpu.make_async_copy(src, dst, sem.at[1 + 3 * n + k])
            copy.start()
            copies.append(copy)
    first.wait()
    for copy in copies:
        copy.wait()


def local(density, mom_r, mom_phi, potential_kernel, force_kernel):
    tables = jnp.asarray(mode_tables())
    rows, lanes = (jnp.asarray(table) for table in row_tables())
    operands = (density, mom_r, mom_phi, potential_kernel, force_kernel, tables, rows, lanes)
    hbm = pl.BlockSpec(memory_space=pltpu.HBM)
    vmem = pl.BlockSpec(memory_space=pltpu.VMEM)
    dma = pltpu.SemaphoreType.DMA
    shared = (
        ((AZ, 8, ROWS), F32),
        ((3, LAYERS, ROWS, CELLS), F32),
        ((3, LAYERS, ROWS + 16, CELLS), F32),
        ((4, 128, CELLS), BF16),
        ((ROWS, 128), F32),
    )
    coef, part, fluid, tab, rtab = pl.pallas_call(
        exchange,
        out_shape=[pltpu.VMEM(shape, dtype) for shape, dtype in shared],
        in_specs=[hbm] * 8,
        out_specs=[vmem] * 5,
        scratch_shapes=[
            pltpu.VMEM((2, 2, ROWS, NR), BF16),
            pltpu.VMEM((8, ROWS), F32),
            pltpu.VMEM((2, ROWS, CELLS), BF16),
            pltpu.VMEM((HALF, 8, ROWS), F32),
            pltpu.VMEM((15, 8, ROWS), F32),
            pltpu.VMEM((2, 8, 128), F32),
            pltpu.VMEM((2, RAD, 8, 128), F32),
            pltpu.VMEM((2, 8, ROWS), F32),
            pltpu.VMEM((2, 8, ROWS), F32),
            pltpu.VMEM((8, ROWS), F32),
            pltpu.VMEM((2, 8, CELLS), F32),
            pltpu.VMEM((2, 8, CELLS), F32),
            pltpu.VMEM((3, LAYERS, 8, CELLS), F32),
            dma((8,)),
            dma((5,)),
            dma((4,)),
            dma((RAD,)),
            dma((5,)),
            dma((5,)),
        ],
        compiler_params=pltpu.CompilerParams(
            collective_id=0, has_side_effects=True, vmem_limit_bytes=32 * 2**20
        ),
        name="exchange",
    )(*(pltpu.with_memory_space_constraint(a, pltpu.HBM) for a in operands))
    fluid_shape = jax.ShapeDtypeStruct((LAYERS, ROWS, CELLS), F32)
    return pl.pallas_call(
        finish,
        out_shape=[fluid_shape, fluid_shape, fluid_shape, jax.ShapeDtypeStruct((ROWS, CELLS), F32)],
        in_specs=[vmem] * 5,
        out_specs=[hbm] * 4,
        scratch_shapes=[
            pltpu.VMEM((ROWS, CELLS), F32),
            pltpu.VMEM((2, LAYERS, ROWS, CELLS), F32),
            dma((1 + 3 * 4,)),
        ],
        compiler_params=pltpu.CompilerParams(vmem_limit_bytes=32 * 2**20),
        name="finish",
    )(coef, part, fluid, tab, rtab)


def solution(mesh):
    fluid = P(None, "rad", "az")
    kernel = P("az", "rad", None)
    return jax.shard_map(
        local,
        mesh=mesh,
        in_specs=(fluid, fluid, fluid, kernel, kernel),
        out_specs=(fluid, fluid, fluid, P("rad", "az")),
        check_vma=False,
    )
```

```python
import math

import jax
import jax.numpy as jnp
import ml_dtypes
import numpy as np
from jax import lax
from jax.experimental import pallas as pl
from jax.experimental.pallas import tpu as pltpu
from jax.sharding import PartitionSpec as P

NR = 2048
NAZ = 16384
MODES = 64
AZ = 32
RAD = 8
HALF = 16
LAYERS = 2
ROWS = NR // RAD
CELLS = NAZ // AZ
STEP = 2.0 * math.pi / NAZ
ASPECT_SQ = 0.0025
MESH = pl.DeviceIdType.MESH
F32 = jnp.float32
BF16 = jnp.bfloat16
NT = (((1,), (1,)), ((), ()))
NN = (((1,), (0,)), ((), ()))


def split(table):
    high = table.astype(ml_dtypes.bfloat16)
    low = (table - high.astype(np.float64)).astype(ml_dtypes.bfloat16)
    return (high, low)


def mode_tables():
    p, h, j = np.meshgrid(np.arange(16), np.arange(2), np.arange(4), indexing="ij")
    column = 4 * (16 * h + p) + j
    mode = (column // 2).astype(np.float64)[..., None]
    odd = (column % 2).astype(bool)[..., None]
    angle = mode * ((np.arange(NAZ) + 0.5) * STEP)
    cos, sin = np.cos(angle), np.sin(angle)
    basis = np.where(odd, sin, cos)
    slope = np.where(odd, mode * cos, -mode * sin)
    analysis = np.stack(split(basis)).reshape(2, 128, AZ, CELLS).transpose(2, 0, 1, 3)
    synthesis = np.stack([split(basis), split(slope)]).transpose(0, 1, 3, 2, 4, 5)
    synthesis = synthesis.reshape(2, 2, 2, 64, AZ, CELLS).transpose(4, 2, 0, 1, 3, 5)
    return (np.ascontiguousarray(analysis), np.ascontiguousarray(synthesis))


def row_tables():
    face = np.exp(np.arange(NR + 1) * STEP)
    inner, outer = face[:-1], face[1:]
    mid = 0.5 * (inner + outer)
    area = 0.5 * (outer * outer - inner * inner)
    table = np.zeros((NR, 128), np.float32)
    columns = [
        ASPECT_SQ / outer,
        np.sqrt(ASPECT_SQ / outer),
        0.05 * STEP * outer / area,
        0.05 * STEP * inner / area,
        ASPECT_SQ / mid,
        np.sqrt(ASPECT_SQ / mid),
        0.05 / mid,
        0.1 * STEP / mid,
        0.1 * STEP * (ASPECT_SQ / mid / mid - 1.0 / (mid * mid)),
        -0.1 / mid,
        ASPECT_SQ / inner,
        np.sqrt(ASPECT_SQ / inner),
    ]
    for k, values in enumerate(columns):
        table[:, k] = values
    across = np.zeros((8, NR), np.float32)
    for k, n in enumerate((4, 5, 6)):
        across[k] = columns[n]
    return (table, across)


def face_flux(low, high, sound, sound_root, pressed):
    rho_l, mr_l, mp_l, v_l = low
    rho_h, mr_h, mp_h, v_h = high
    speed = jnp.maximum(jnp.abs(v_l), jnp.abs(v_h)) + sound_root
    a, b = v_l + speed, v_h - speed
    flux = [rho_l * a + rho_h * b, mr_l * a + mr_h * b, mp_l * a + mp_h * b]
    flux[pressed] = flux[pressed] + sound * (rho_l + rho_h)
    return flux


def reciprocal(value):
    guess = pl.reciprocal(value, approx=True)
    return guess * (2.0 - value * guess)


def whole(ref, count):
    slots = ref.at[pl.ds(0, count)]
    return lambda sem: pltpu.make_async_copy(slots, slots, sem).wait()


def radial_flux(low, high, sound, sound_root):
    return face_flux(
        (*low, low[1] * reciprocal(low[0])),
        (*high, high[1] * reciprocal(high[0])),
        sound,
        sound_root,
        1,
    )


def azimuth_flux(low, high, sound, sound_root):
    return face_flux(
        (*low, low[2] * reciprocal(low[0])),
        (*high, high[2] * reciprocal(high[0])),
        sound,
        sound_root,
        2,
    )


def pairs_of(ref, at):
    value = ref[at]
    return [value[2 * c : 2 * c + 2] for c in range(3)]


def stacked(tiles):
    value = jnp.concatenate(tiles, axis=0)
    high = value.astype(BF16).astype(F32)
    return jnp.concatenate([high, high, value - high], axis=0).T.astype(BF16)


def synthesis(coef, half, syn, sides):
    row_id = lax.broadcasted_iota(jnp.int32, (8, ROWS), 0)
    pots, forces = [], []
    for n in range(0, HALF, 2):
        a, b = coef[half * HALF + n], coef[half * HALF + n + 1]
        pots.append(jnp.where(row_id < 4, a, pltpu.roll(b, 4, 0)))
        forces.append(jnp.where(row_id < 4, pltpu.roll(a, 4, 0), b))
    sides[0] = stacked(pots)
    sides[1] = stacked(forces)

    def product(here, side, table):
        weights = syn[half, table].reshape(192, CELLS)
        return lax.dot_general(sides[side, here, :], weights, NN, preferred_element_type=F32)

    def at(here, rtab):
        radial = 0.1 * product(here, 1, 0)
        azimuthal = product(here, 0, 1) * rtab[here, 9:10]
        return product(here, 0, 0), radial, azimuthal

    return at


def exchange(
    density,
    mom_r,
    mom_phi,
    pot_kernel,
    force_kernel,
    analysis,
    tables,
    rows,
    lanes,
    coef,
    part,
    fluid,
    syn,
    rtab,
    pot,
    tab,
    sides,
    kern,
    ltab,
    surf,
    chunks,
    arrived,
    halfsum,
    gathered,
    az_out,
    az_in,
    az_swap,
    rad_out,
    rad_in,
    carry,
    load_sem,
    send_sem,
    recv_sem,
    column_sem,
    edge_send,
    edge_recv,
):
    az = lax.axis_index("az")
    rad = lax.axis_index("rad")
    z_hi = az // HALF
    p = az % HALF
    y, x = p // 4, p % 4
    z, core = z_hi * 4 + rad // 2, rad % 2
    q = z_hi * RAD + rad
    partner = ((az + HALF) % AZ, rad)

    far = [(2, 2), (1, 2), (2, 1), (3, 2), (2, 3), (1, 1), (3, 3), (1, 3), (3, 1), (2, 0), (0, 2), (0, 1), (1, 0), (0, 3), (3, 0)]
    plane = [(y + dy) % 4 * 4 + (x + dx) % 4 for dy, dx in far]
    column = []
    for dz, dc in [(4, 0), (4, 1), (3, 0), (5, 0), (3, 1), (5, 1), (2, 0), (6, 0), (2, 1), (6, 1), (1, 0), (7, 0), (1, 1), (7, 1), (0, 1)]:
        there = (z + dz) % 8
        column.append((there // 4, there % 4 * 2 + (core + dc) % 2))

    barrier = pltpu.get_barrier_semaphore()
    for to in plane:
        pl.semaphore_signal(barrier, inc=1, device_id=(z_hi * HALF + to, rad), device_id_type=MESH)
    for half, to in column:
        pl.semaphore_signal(barrier, inc=1, device_id=(half * HALF + p, to), device_id_type=MESH)

    inside = pl.ds(8, ROWS)
    loads = [
        pltpu.make_async_copy(density, fluid.at[0, :, inside, :], load_sem.at[0]),
        pltpu.make_async_copy(analysis.at[az], tab, load_sem.at[1]),
        pltpu.make_async_copy(mom_r, fluid.at[1, :, inside, :], load_sem.at[2]),
        pltpu.make_async_copy(mom_phi, fluid.at[2, :, inside, :], load_sem.at[3]),
        pltpu.make_async_copy(rows.at[pl.ds(rad * ROWS, ROWS), :], rtab, load_sem.at[4]),
        pltpu.make_async_copy(lanes.at[:, pl.ds(rad * ROWS, ROWS)], ltab, load_sem.at[5]),
        pltpu.make_async_copy(pot_kernel, kern.at[0], load_sem.at[6]),
        pltpu.make_async_copy(force_kernel, kern.at[1], load_sem.at[7]),
        pltpu.make_async_copy(tables.at[az], syn.at[:, :, pl.ds(0, 2)], load_sem.at[8]),
        pltpu.make_async_copy(tables.at[az, :, :, 0], syn.at[:, :, 2], load_sem.at[9]),
    ]
    for load in loads:
        load.start()

    loads[0].wait()

    @pl.loop(0, ROWS // 32)
    def _(block):
        at = pl.multiple_of(block * 32, 32)
        value = fluid[0, 0, pl.ds(8 + at, 32), :] + fluid[0, 1, pl.ds(8 + at, 32), :]
        high = value.astype(BF16)
        surf[0, pl.ds(at, 32), :] = high
        surf[1, pl.ds(at, 32), :] = (value - high.astype(F32)).astype(BF16)

    loads[1].wait()
    share = lax.dot_general(tab[0], surf[0], NT, preferred_element_type=F32)
    share += lax.dot_general(tab[0], surf[1], NT, preferred_element_type=F32)
    share += lax.dot_general(tab[1], surf[0], NT, preferred_element_type=F32)
    chunks[...] = share.reshape(HALF, 8, ROWS)

    pl.semaphore_wait(barrier, len(plane) + len(column))

    for k, to in enumerate(plane):
        pltpu.make_async_remote_copy(
            src_ref=chunks.at[to],
            dst_ref=arrived.at[k],
            send_sem=send_sem.at[0],
            recv_sem=recv_sem.at[0],
            device_id=(z_hi * HALF + to, rad),
            device_id_type=MESH,
        ).start()

    loads[2].wait()
    loads[3].wait()
    row_id = lax.broadcasted_iota(jnp.int32, (8, 256), 0)
    lane_id = lax.broadcasted_iota(jnp.int32, (8, 256), 1)
    for side, (at, lane) in enumerate(((0, 0), (CELLS - 128, 127))):
        total = jnp.zeros((8, ROWS), F32)
        for c in range(3):
            both = jnp.concatenate([fluid[c, n, inside, at : at + 128] for n in range(2)], axis=1)
            pick = jnp.where(lane_id == lane + 128 * (row_id - 2 * c), 1.0, 0.0)
            pick = jnp.where((row_id == 2 * c) | (row_id == 2 * c + 1), pick, 0.0).astype(BF16)
            high = both.astype(BF16)
            low = (both - high.astype(F32)).astype(BF16)
            total += lax.dot_general(pick, high, NT, preferred_element_type=F32)
            total += lax.dot_general(pick, low, NT, preferred_element_type=F32)
        az_out[side] = total
    rad_out[...] = jnp.zeros_like(rad_out)
    for f in range(6):
        rad_out[0, f : f + 1, :] = fluid[f // 2, f % 2, 8:9, :]
        rad_out[1, f : f + 1, :] = fluid[f // 2, f % 2, 8 + ROWS - 1 : 8 + ROWS, :]
    edges = []
    for n, (src, dst, device) in enumerate(
        (
            (az_out.at[0], az_in.at[1], (z_hi * HALF + (p + HALF - 1) % HALF, rad)),
            (az_out.at[1], az_in.at[0], (z_hi * HALF + (p + 1) % HALF, rad)),
            (rad_out.at[0], rad_in.at[1], (az, (rad + RAD - 1) % RAD)),
            (rad_out.at[1], rad_in.at[0], (az, (rad + 1) % RAD)),
        )
    ):
        copy = pltpu.make_async_remote_copy(
            src_ref=src,
            dst_ref=dst,
            send_sem=edge_send.at[n],
            recv_sem=edge_recv.at[n],
            device_id=device,
            device_id_type=MESH,
        )
        copy.start()
        edges.append(copy)

    loads[4].wait()
    for c in range(3):
        for layer in range(LAYERS):
            fluid[c, layer, 0:8, :] = jnp.broadcast_to(fluid[c, layer, 8:9, :], (8, CELLS))
            fluid[c, layer, 8 + ROWS : 16 + ROWS, :] = jnp.broadcast_to(
                fluid[c, layer, 7 + ROWS : 8 + ROWS, :], (8, CELLS)
            )
    for layer in range(LAYERS):
        edge = [fluid[c, layer, 0:8, :] for c in range(3)]
        flux = radial_flux(edge, edge, rtab[0:1, 10:11], rtab[0:1, 11:12])
        for c in range(3):
            carry[c, layer] = flux[c]

    size = 32

    def update(block):
        at = pl.multiple_of(block * size, size)
        here = pl.ds(at, size)

        def factor(k):
            return jnp.broadcast_to(rtab[here, k : k + 1], (size, CELLS))

        for layer in range(LAYERS):
            state = [fluid[c, layer, pl.ds(at + 8, size + 8), :] for c in range(3)]
            inv = reciprocal(state[0])
            state.append(state[1] * inv)
            low = [value[:size] for value in state]
            high = [pltpu.roll(value, size + 7, 0)[:size] for value in state]
            flux = face_flux(low, high, factor(0), factor(1), 1)
            rho, mr, mp = low[:3]
            vp = mp * inv[:size]
            cells = (rho, mr, mp, vp)
            left = [pltpu.roll(value, 1, 1) for value in cells]
            side = face_flux(left, cells, factor(4), factor(5), 2)
            new = []
            for c in range(3):
                below = pltpu.roll(jnp.concatenate([carry[c, layer], flux[c]], axis=0), 1, 0)[8:]
                above = pltpu.roll(side[c], CELLS - 1, 1)
                carry[c, layer] = flux[c][size - 8 :]
                new.append(
                    low[c]
                    - (factor(2) * flux[c] - factor(3) * below + factor(6) * (above - side[c]))
                )
            turn = factor(7) * vp
            new[1] = new[1] + (turn * mp + factor(8) * rho)
            new[2] = new[2] - turn * mr
            for c in range(3):
                part[c, layer, here, :] = new[c]

    early = 4
    pl.loop(0, early)(update)

    whole(arrived, 15)(recv_sem.at[0])
    total = chunks[p]
    for k in range(15):
        total = total + arrived[k]
    for h in range(2):
        halfsum[h, 0:4, :] = total[4 * h : 4 * h + 4, 0:128]
        halfsum[h, 4:8, :] = total[4 * h : 4 * h + 4, 128:256]
    gathered[z_hi, rad] = halfsum[z_hi]
    for half, to in column:
        pltpu.make_async_remote_copy(
            src_ref=halfsum.at[half],
            dst_ref=gathered.at[z_hi, rad],
            send_sem=send_sem.at[1],
            recv_sem=column_sem.at[(rad - to + RAD) % RAD],
            device_id=(half * HALF + p, to),
            device_id_type=MESH,
        ).start()

    pl.loop(early, ROWS // size)(update)

    edges[2].wait()
    edges[3].wait()
    for side, (outermost, sign, weight, sound) in enumerate(
        ((rad == 0, 1.0, rtab[0:1, 3:4], 10), (rad == RAD - 1, -1.0, rtab[ROWS - 1 : ROWS, 2:3], 0))
    ):
        row = 0 if side == 0 else ROWS - 1
        sounds = (rtab[row : row + 1, sound : sound + 1], rtab[row : row + 1, sound + 1 : sound + 2])
        own = pairs_of(rad_out, side)
        beyond = [jnp.where(outermost, a, b) for a, b in zip(own, pairs_of(rad_in, side))]
        used = radial_flux(own, own, *sounds)
        right = radial_flux(beyond, own, *sounds) if side == 0 else radial_flux(own, beyond, *sounds)
        for c in range(3):
            delta = (sign * weight) * (right[c] - used[c])
            for layer in range(LAYERS):
                part[c, layer, row : row + 1, :] = part[c, layer, row : row + 1, :] + delta[layer : layer + 1]

    edges[0].wait()
    edges[1].wait()
    end = p // (HALF - 1)
    swap = pltpu.make_async_remote_copy(
        src_ref=az_in.at[end],
        dst_ref=az_swap,
        send_sem=edge_send.at[4],
        recv_sem=edge_recv.at[4],
        device_id=partner,
        device_id_type=MESH,
    )
    at_end = (p == 0) | (p == HALF - 1)

    @pl.when(at_end)
    def _():
        swap.start()

    loads[6].wait()
    loads[7].wait()
    products = [jnp.zeros((16, ROWS), F32) for _ in range(4)]
    for k in (0, 1, 7, 2, 6, 3, 5, 4):
        from_rad = (rad + k) % RAD
        pair = gathered.at[:, from_rad] if k else gathered.at[pl.ds(0, 1), from_rad]
        pltpu.make_async_copy(pair, pair, column_sem.at[k]).wait()
        both = (gathered[0, from_rad] + gathered[1, from_rad]) * (1.0 / NAZ)
        modes = jnp.concatenate([both[0:4], both[4:8]], axis=1)
        modes = jnp.concatenate([modes] * 4, axis=0).astype(BF16)
        at = pl.ds(pl.multiple_of(from_rad * ROWS, ROWS), ROWS)
        for n in range(4):
            products[n] += lax.dot_general(modes, kern[n // 2, n % 2, :, at], NT, preferred_element_type=F32)
    for n in range(4):
        m = n % 2
        coef[az, 2 * n : 2 * n + 2, :] = products[n][2 * m : 2 * m + 2]

    def to_plane(slot, n):
        for to in plane:
            pltpu.make_async_remote_copy(
                src_ref=coef.at[slot],
                dst_ref=coef.at[slot],
                send_sem=send_sem.at[1 + n],
                recv_sem=recv_sem.at[n],
                device_id=(z_hi * HALF + to, rad),
                device_id_type=MESH,
            ).start()

    cross = pltpu.make_async_remote_copy(
        src_ref=coef.at[az],
        dst_ref=coef.at[az],
        send_sem=send_sem.at[2],
        recv_sem=recv_sem.at[1],
        device_id=partner,
        device_id_type=MESH,
    )

    direct = rad < RAD // 2
    far_sends = direct & (z_hi == 1)
    far_receives = direct & (z_hi == 0)

    @pl.when(jnp.logical_not(far_sends))
    def _():
        cross.start()

    @pl.when(far_sends)
    def _():
        for to in plane + [p]:
            pltpu.make_async_remote_copy(
                src_ref=coef.at[az],
                dst_ref=coef.at[az],
                send_sem=send_sem.at[2],
                recv_sem=recv_sem.at[3],
                device_id=(to, rad),
                device_id_type=MESH,
            ).start()

    to_plane(az, 2)

    @pl.when(at_end)
    def _():
        swap.wait()
        az_in[end] = az_swap[...]

    loads[5].wait()
    own_low, own_high = pairs_of(az_out, 0), pairs_of(az_out, 1)
    sounds = (ltab[0:1, :], ltab[1:2, :])
    used = azimuth_flux(own_high, own_low, *sounds)
    below = azimuth_flux(pairs_of(az_in, 0), own_low, *sounds)
    above = azimuth_flux(own_high, pairs_of(az_in, 1), *sounds)
    blank = jnp.zeros((2, ROWS), F32)
    weight = ltab[2:3, :]
    first = jnp.concatenate([weight * (a - b) for a, b in zip(below, used)] + [blank], axis=0)
    last = jnp.concatenate([weight * (b - a) for a, b in zip(above, used)] + [blank], axis=0)
    lane_id = lax.broadcasted_iota(jnp.int32, (ROWS, 128), 1)
    for at, lane, rim in ((0, 0, first.T), (CELLS - 128, 127, last.T)):
        for f in range(6):
            here = (f // 2, f % 2, slice(None), pl.ds(at, 128))
            delta = jnp.broadcast_to(rim[:, f : f + 1], (ROWS, 128))
            part[here] = part[here] + jnp.where(lane_id == lane, delta, 0.0)

    @pl.when(jnp.logical_not(far_receives))
    def _():
        cross.wait_recv()
        to_plane(partner[0], 3)

    whole(coef, 15)(recv_sem.at[2])
    loads[8].wait()
    loads[9].wait()
    gravity = synthesis(coef, z_hi, syn, sides)
    block = 32

    @pl.loop(0, ROWS // block)
    def _(n):
        first_row = pl.multiple_of(n * block, block)
        here = pl.ds(first_row, block)
        potential, radial, azimuthal = gravity(here, rtab)
        pot[here, :] = potential
        for layer in range(LAYERS):
            rho = fluid[0, layer, pl.ds(first_row + 8, block), :]
            part[1, layer, here, :] = part[1, layer, here, :] + rho * radial
            part[2, layer, here, :] = part[2, layer, here, :] + rho * azimuthal

    @pl.when(far_receives)
    def _():
        whole(coef, 16)(recv_sem.at[3])

    @pl.when(jnp.logical_not(far_receives))
    def _():
        whole(coef, 15)(recv_sem.at[3])
        whole(coef, 15)(send_sem.at[4])

    @pl.when(far_sends)
    def _():
        whole(coef, 16)(send_sem.at[2])

    @pl.when(jnp.logical_not(far_sends))
    def _():
        cross.wait_send()

    for n in (0, 3):
        whole(coef, 15)(send_sem.at[n])
    whole(coef.at[:, :, pl.ds(0, 128)], 15)(send_sem.at[1])


def finish(coef, part, fluid, syn, rtab, pot, out_density, out_r, out_phi, out_pot, sides, pot_buf, mom_buf, sem):
    first = pltpu.make_async_copy(part.at[0], out_density, sem.at[0])
    first.start()
    gravity = synthesis(coef, 1 - lax.axis_index("az") // HALF, syn, sides)
    block = 64
    copies = []
    for n in range(ROWS // block):
        here = slice(n * block, (n + 1) * block)
        potential, radial, azimuthal = gravity(here, rtab)
        pot_buf[here, :] = pot[here, :] + potential
        inside = slice(8 + n * block, 8 + (n + 1) * block)
        for layer in range(LAYERS):
            rho = fluid[0, layer, inside, :]
            mom_buf[0, layer, here, :] = part[1, layer, here, :] + rho * radial
            mom_buf[1, layer, here, :] = part[2, layer, here, :] + rho * azimuthal
        rows = pl.ds(n * block, block)
        for k, (src, dst) in enumerate(
            (
                (pot_buf.at[rows, :], out_pot.at[rows, :]),
                (mom_buf.at[0, :, rows, :], out_r.at[:, rows, :]),
                (mom_buf.at[1, :, rows, :], out_phi.at[:, rows, :]),
            )
        ):
            copy = pltpu.make_async_copy(src, dst, sem.at[1 + 3 * n + k])
            copy.start()
            copies.append(copy)
    first.wait()
    for copy in copies:
        copy.wait()


def local(density, mom_r, mom_phi, potential_kernel, force_kernel):
    analysis, tables = (jnp.asarray(table) for table in mode_tables())
    rows, lanes = (jnp.asarray(table) for table in row_tables())
    operands = (density, mom_r, mom_phi, potential_kernel, force_kernel, analysis, tables, rows, lanes)
    hbm = pl.BlockSpec(memory_space=pltpu.HBM)
    vmem = pl.BlockSpec(memory_space=pltpu.VMEM)
    dma = pltpu.SemaphoreType.DMA
    shared = (
        ((AZ, 8, ROWS), F32),
        ((3, LAYERS, ROWS, CELLS), F32),
        ((3, LAYERS, ROWS + 16, CELLS), F32),
        ((2, 2, 3, 64, CELLS), BF16),
        ((ROWS, 128), F32),
        ((ROWS, CELLS), F32),
    )
    shared = pl.pallas_call(
        exchange,
        out_shape=[pltpu.VMEM(shape, dtype) for shape, dtype in shared],
        in_specs=[hbm] * 9,
        out_specs=[vmem] * 6,
        scratch_shapes=[
            pltpu.VMEM((2, 128, CELLS), BF16),
            pltpu.VMEM((2, ROWS, 192), BF16),
            pltpu.VMEM((2, 2, ROWS, NR), BF16),
            pltpu.VMEM((8, ROWS), F32),
            pltpu.VMEM((2, ROWS, CELLS), BF16),
            pltpu.VMEM((HALF, 8, ROWS), F32),
            pltpu.VMEM((15, 8, ROWS), F32),
            pltpu.VMEM((2, 8, 128), F32),
            pltpu.VMEM((2, RAD, 8, 128), F32),
            pltpu.VMEM((2, 8, ROWS), F32),
            pltpu.VMEM((2, 8, ROWS), F32),
            pltpu.VMEM((8, ROWS), F32),
            pltpu.VMEM((2, 8, CELLS), F32),
            pltpu.VMEM((2, 8, CELLS), F32),
            pltpu.VMEM((3, LAYERS, 8, CELLS), F32),
            dma((10,)),
            dma((5,)),
            dma((4,)),
            dma((RAD,)),
            dma((5,)),
            dma((5,)),
        ],
        compiler_params=pltpu.CompilerParams(
            collective_id=0, has_side_effects=True, vmem_limit_bytes=32 * 2**20
        ),
        name="exchange",
    )(*(pltpu.with_memory_space_constraint(a, pltpu.HBM) for a in operands))
    fluid_shape = jax.ShapeDtypeStruct((LAYERS, ROWS, CELLS), F32)
    return pl.pallas_call(
        finish,
        out_shape=[fluid_shape, fluid_shape, fluid_shape, jax.ShapeDtypeStruct((ROWS, CELLS), F32)],
        in_specs=[vmem] * 6,
        out_specs=[hbm] * 4,
        scratch_shapes=[
            pltpu.VMEM((2, ROWS, 192), BF16),
            pltpu.VMEM((ROWS, CELLS), F32),
            pltpu.VMEM((2, LAYERS, ROWS, CELLS), F32),
            dma((1 + 3 * 4,)),
        ],
        compiler_params=pltpu.CompilerParams(vmem_limit_bytes=32 * 2**20),
        name="finish",
    )(*shared)


def solution(mesh):
    fluid = P(None, "rad", "az")
    kernel = P("az", "rad", None)
    return jax.shard_map(
        local,
        mesh=mesh,
        in_specs=(fluid, fluid, fluid, kernel, kernel),
        out_specs=(fluid, fluid, fluid, P("rad", "az")),
        check_vma=False,
    )
```

```python
import math

import jax
import jax.numpy as jnp
import ml_dtypes
import numpy as np
from jax import lax
from jax.experimental import pallas as pl
from jax.experimental.pallas import tpu as pltpu
from jax.sharding import PartitionSpec as P

NR = 2048
NAZ = 16384
MODES = 64
AZ = 32
RAD = 8
HALF = 16
LAYERS = 2
ROWS = NR // RAD
CELLS = NAZ // AZ
STEP = 2.0 * math.pi / NAZ
ASPECT_SQ = 0.0025
MESH = pl.DeviceIdType.MESH
F32 = jnp.float32
BF16 = jnp.bfloat16
NT = (((1,), (1,)), ((), ()))
NN = (((1,), (0,)), ((), ()))


def split(table):
    high = table.astype(ml_dtypes.bfloat16)
    low = (table - high.astype(np.float64)).astype(ml_dtypes.bfloat16)
    return (high, low)


def mode_tables():
    p, h, j = np.meshgrid(np.arange(16), np.arange(2), np.arange(4), indexing="ij")
    column = 4 * (16 * h + p) + j
    mode = (column // 2).astype(np.float64)[..., None]
    odd = (column % 2).astype(bool)[..., None]
    angle = mode * ((np.arange(NAZ) + 0.5) * STEP)
    cos, sin = np.cos(angle), np.sin(angle)
    basis = np.where(odd, sin, cos)
    slope = np.where(odd, mode * cos, -mode * sin)
    analysis = np.stack(split(basis)).reshape(2, 128, AZ, CELLS).transpose(2, 0, 1, 3)
    synthesis = np.stack([split(basis), split(slope)]).transpose(0, 1, 3, 2, 4, 5)
    synthesis = synthesis.reshape(2, 2, 2, 64, AZ, CELLS).transpose(4, 2, 0, 1, 3, 5)
    return (np.ascontiguousarray(analysis), np.ascontiguousarray(synthesis))


def row_tables():
    face = np.exp(np.arange(NR + 1) * STEP)
    inner, outer = face[:-1], face[1:]
    mid = 0.5 * (inner + outer)
    area = 0.5 * (outer * outer - inner * inner)
    table = np.zeros((NR, 128), np.float32)
    columns = [
        ASPECT_SQ / outer,
        np.sqrt(ASPECT_SQ / outer),
        0.05 * STEP * outer / area,
        0.05 * STEP * inner / area,
        ASPECT_SQ / mid,
        np.sqrt(ASPECT_SQ / mid),
        0.05 / mid,
        0.1 * STEP / mid,
        0.1 * STEP * (ASPECT_SQ / mid / mid - 1.0 / (mid * mid)),
        -0.1 / mid,
        ASPECT_SQ / inner,
        np.sqrt(ASPECT_SQ / inner),
    ]
    for k, values in enumerate(columns):
        table[:, k] = values
    across = np.zeros((8, NR), np.float32)
    for k, n in enumerate((4, 5, 6)):
        across[k] = columns[n]
    return (table, across)


def face_flux(low, high, sound, sound_root, pressed):
    rho_l, mr_l, mp_l, v_l = low
    rho_h, mr_h, mp_h, v_h = high
    speed = jnp.maximum(jnp.abs(v_l), jnp.abs(v_h)) + sound_root
    a, b = v_l + speed, v_h - speed
    flux = [rho_l * a + rho_h * b, mr_l * a + mr_h * b, mp_l * a + mp_h * b]
    flux[pressed] = flux[pressed] + sound * (rho_l + rho_h)
    return flux


def reciprocal(value):
    guess = pl.reciprocal(value, approx=True)
    return guess * (2.0 - value * guess)


def whole(ref, count):
    slots = ref.at[pl.ds(0, count)]
    return lambda sem: pltpu.make_async_copy(slots, slots, sem).wait()


def radial_flux(low, high, sound, sound_root):
    return face_flux(
        (*low, low[1] * reciprocal(low[0])),
        (*high, high[1] * reciprocal(high[0])),
        sound,
        sound_root,
        1,
    )


def azimuth_flux(low, high, sound, sound_root):
    return face_flux(
        (*low, low[2] * reciprocal(low[0])),
        (*high, high[2] * reciprocal(high[0])),
        sound,
        sound_root,
        2,
    )


def pairs_of(ref, at):
    value = ref[at]
    return [value[2 * c : 2 * c + 2] for c in range(3)]


def stacked(tiles):
    value = jnp.concatenate(tiles, axis=0)
    high = value.astype(BF16).astype(F32)
    return jnp.concatenate([high, high, value - high], axis=0).T.astype(BF16)


def synthesis(coef, half, syn, sides):
    row_id = lax.broadcasted_iota(jnp.int32, (8, ROWS), 0)
    pots, forces = [], []
    for n in range(0, HALF, 2):
        a, b = coef[half * HALF + n], coef[half * HALF + n + 1]
        pots.append(jnp.where(row_id < 4, a, pltpu.roll(b, 4, 0)))
        forces.append(jnp.where(row_id < 4, pltpu.roll(a, 4, 0), b))
    sides[0] = stacked(pots)
    sides[1] = stacked(forces)

    def product(here, side, table):
        weights = syn[half, table].reshape(192, CELLS)
        return lax.dot_general(sides[side, here, :], weights, NN, preferred_element_type=F32)

    def at(here, rtab):
        radial = 0.1 * product(here, 1, 0)
        azimuthal = product(here, 0, 1) * rtab[here, 9:10]
        return product(here, 0, 0), radial, azimuthal

    return at


def exchange(
    density,
    mom_r,
    mom_phi,
    pot_kernel,
    force_kernel,
    analysis,
    tables,
    rows,
    lanes,
    coef,
    part,
    fluid,
    syn,
    rtab,
    pot,
    tab,
    sides,
    kern,
    ltab,
    surf,
    chunks,
    arrived,
    halfsum,
    gathered,
    az_out,
    az_in,
    az_swap,
    rad_out,
    rad_in,
    carry,
    load_sem,
    send_sem,
    recv_sem,
    column_sem,
    edge_send,
    edge_recv,
):
    az = lax.axis_index("az")
    rad = lax.axis_index("rad")
    z_hi = az // HALF
    p = az % HALF
    y, x = p // 4, p % 4
    z, core = z_hi * 4 + rad // 2, rad % 2
    q = z_hi * RAD + rad
    partner = ((az + HALF) % AZ, rad)

    far = [(2, 2), (1, 2), (2, 1), (3, 2), (2, 3), (1, 1), (3, 3), (1, 3), (3, 1), (2, 0), (0, 2), (0, 1), (1, 0), (0, 3), (3, 0)]
    plane = [(y + dy) % 4 * 4 + (x + dx) % 4 for dy, dx in far]
    column = []
    for dz, dc in [(4, 0), (4, 1), (3, 0), (5, 0), (3, 1), (5, 1), (2, 0), (6, 0), (2, 1), (6, 1), (1, 0), (7, 0), (1, 1), (7, 1), (0, 1)]:
        there = (z + dz) % 8
        column.append((there // 4, there % 4 * 2 + (core + dc) % 2))

    barrier = pltpu.get_barrier_semaphore()
    for to in plane:
        pl.semaphore_signal(barrier, inc=1, device_id=(z_hi * HALF + to, rad), device_id_type=MESH)
    for half, to in column:
        pl.semaphore_signal(barrier, inc=1, device_id=(half * HALF + p, to), device_id_type=MESH)

    inside = pl.ds(8, ROWS)
    loads = [
        pltpu.make_async_copy(density, fluid.at[0, :, inside, :], load_sem.at[0]),
        pltpu.make_async_copy(analysis.at[az], tab, load_sem.at[1]),
        pltpu.make_async_copy(mom_r, fluid.at[1, :, inside, :], load_sem.at[2]),
        pltpu.make_async_copy(mom_phi, fluid.at[2, :, inside, :], load_sem.at[3]),
        pltpu.make_async_copy(rows.at[pl.ds(rad * ROWS, ROWS), :], rtab, load_sem.at[4]),
        pltpu.make_async_copy(lanes.at[:, pl.ds(rad * ROWS, ROWS)], ltab, load_sem.at[5]),
        pltpu.make_async_copy(pot_kernel, kern.at[0], load_sem.at[6]),
        pltpu.make_async_copy(force_kernel, kern.at[1], load_sem.at[7]),
        pltpu.make_async_copy(tables.at[az], syn.at[:, :, pl.ds(0, 2)], load_sem.at[8]),
        pltpu.make_async_copy(tables.at[az, :, :, 0], syn.at[:, :, 2], load_sem.at[9]),
    ]
    for load in loads:
        load.start()

    loads[0].wait()

    @pl.loop(0, ROWS // 32)
    def _(block):
        at = pl.multiple_of(block * 32, 32)
        value = fluid[0, 0, pl.ds(8 + at, 32), :] + fluid[0, 1, pl.ds(8 + at, 32), :]
        high = value.astype(BF16)
        surf[0, pl.ds(at, 32), :] = high
        surf[1, pl.ds(at, 32), :] = (value - high.astype(F32)).astype(BF16)

    loads[1].wait()
    share = lax.dot_general(tab[0], surf[0], NT, preferred_element_type=F32)
    share += lax.dot_general(tab[0], surf[1], NT, preferred_element_type=F32)
    share += lax.dot_general(tab[1], surf[0], NT, preferred_element_type=F32)
    chunks[...] = share.reshape(HALF, 8, ROWS)

    pl.semaphore_wait(barrier, len(plane) + len(column))

    for k, to in enumerate(plane):
        pltpu.make_async_remote_copy(
            src_ref=chunks.at[to],
            dst_ref=arrived.at[k],
            send_sem=send_sem.at[0],
            recv_sem=recv_sem.at[0],
            device_id=(z_hi * HALF + to, rad),
            device_id_type=MESH,
        ).start()

    loads[2].wait()
    loads[3].wait()
    row_id = lax.broadcasted_iota(jnp.int32, (8, 256), 0)
    lane_id = lax.broadcasted_iota(jnp.int32, (8, 256), 1)
    for side, (at, lane) in enumerate(((0, 0), (CELLS - 128, 127))):
        total = jnp.zeros((8, ROWS), F32)
        for c in range(3):
            both = jnp.concatenate([fluid[c, n, inside, at : at + 128] for n in range(2)], axis=1)
            pick = jnp.where(lane_id == lane + 128 * (row_id - 2 * c), 1.0, 0.0)
            pick = jnp.where((row_id == 2 * c) | (row_id == 2 * c + 1), pick, 0.0).astype(BF16)
            high = both.astype(BF16)
            low = (both - high.astype(F32)).astype(BF16)
            total += lax.dot_general(pick, high, NT, preferred_element_type=F32)
            total += lax.dot_general(pick, low, NT, preferred_element_type=F32)
        az_out[side] = total
    rad_out[...] = jnp.zeros_like(rad_out)
    for f in range(6):
        rad_out[0, f : f + 1, :] = fluid[f // 2, f % 2, 8:9, :]
        rad_out[1, f : f + 1, :] = fluid[f // 2, f % 2, 8 + ROWS - 1 : 8 + ROWS, :]
    edges = []
    for n, (src, dst, device) in enumerate(
        (
            (az_out.at[0], az_in.at[1], (z_hi * HALF + (p + HALF - 1) % HALF, rad)),
            (az_out.at[1], az_in.at[0], (z_hi * HALF + (p + 1) % HALF, rad)),
            (rad_out.at[0], rad_in.at[1], (az, (rad + RAD - 1) % RAD)),
            (rad_out.at[1], rad_in.at[0], (az, (rad + 1) % RAD)),
        )
    ):
        copy = pltpu.make_async_remote_copy(
            src_ref=src,
            dst_ref=dst,
            send_sem=edge_send.at[n],
            recv_sem=edge_recv.at[n],
            device_id=device,
            device_id_type=MESH,
        )
        copy.start()
        edges.append(copy)

    loads[4].wait()
    for c in range(3):
        for layer in range(LAYERS):
            fluid[c, layer, 0:8, :] = jnp.broadcast_to(fluid[c, layer, 8:9, :], (8, CELLS))
            fluid[c, layer, 8 + ROWS : 16 + ROWS, :] = jnp.broadcast_to(
                fluid[c, layer, 7 + ROWS : 8 + ROWS, :], (8, CELLS)
            )
    for layer in range(LAYERS):
        edge = [fluid[c, layer, 0:8, :] for c in range(3)]
        flux = radial_flux(edge, edge, rtab[0:1, 10:11], rtab[0:1, 11:12])
        for c in range(3):
            carry[c, layer] = flux[c]

    size = 32

    def update(block):
        at = pl.multiple_of(block * size, size)
        here = pl.ds(at, size)

        def factor(k):
            return jnp.broadcast_to(rtab[here, k : k + 1], (size, CELLS))

        for layer in range(LAYERS):
            state = [fluid[c, layer, pl.ds(at + 8, size + 8), :] for c in range(3)]
            inv = reciprocal(state[0])
            state.append(state[1] * inv)
            low = [value[:size] for value in state]
            high = [pltpu.roll(value, size + 7, 0)[:size] for value in state]
            flux = face_flux(low, high, factor(0), factor(1), 1)
            rho, mr, mp = low[:3]
            vp = mp * inv[:size]
            cells = (rho, mr, mp, vp)
            left = [pltpu.roll(value, 1, 1) for value in cells]
            side = face_flux(left, cells, factor(4), factor(5), 2)
            new = []
            for c in range(3):
                below = pltpu.roll(jnp.concatenate([carry[c, layer], flux[c]], axis=0), 1, 0)[8:]
                above = pltpu.roll(side[c], CELLS - 1, 1)
                carry[c, layer] = flux[c][size - 8 :]
                new.append(
                    low[c]
                    - (factor(2) * flux[c] - factor(3) * below + factor(6) * (above - side[c]))
                )
            turn = factor(7) * vp
            new[1] = new[1] + (turn * mp + factor(8) * rho)
            new[2] = new[2] - turn * mr
            for c in range(3):
                part[c, layer, here, :] = new[c]

    early = 4
    pl.loop(0, early)(update)

    whole(arrived, 15)(recv_sem.at[0])
    total = chunks[p]
    for k in range(15):
        total = total + arrived[k]
    for h in range(2):
        halfsum[h, 0:4, :] = total[4 * h : 4 * h + 4, 0:128]
        halfsum[h, 4:8, :] = total[4 * h : 4 * h + 4, 128:256]
    gathered[z_hi, rad] = halfsum[z_hi]
    for half, to in column:
        pltpu.make_async_remote_copy(
            src_ref=halfsum.at[half],
            dst_ref=gathered.at[z_hi, rad],
            send_sem=send_sem.at[1],
            recv_sem=column_sem.at[(rad - to + RAD) % RAD],
            device_id=(half * HALF + p, to),
            device_id_type=MESH,
        ).start()

    pl.loop(early, ROWS // size)(update)

    edges[2].wait()
    edges[3].wait()
    for side, (outermost, sign, weight, sound) in enumerate(
        ((rad == 0, 1.0, rtab[0:1, 3:4], 10), (rad == RAD - 1, -1.0, rtab[ROWS - 1 : ROWS, 2:3], 0))
    ):
        row = 0 if side == 0 else ROWS - 1
        sounds = (rtab[row : row + 1, sound : sound + 1], rtab[row : row + 1, sound + 1 : sound + 2])
        own = pairs_of(rad_out, side)
        beyond = [jnp.where(outermost, a, b) for a, b in zip(own, pairs_of(rad_in, side))]
        used = radial_flux(own, own, *sounds)
        right = radial_flux(beyond, own, *sounds) if side == 0 else radial_flux(own, beyond, *sounds)
        for c in range(3):
            delta = (sign * weight) * (right[c] - used[c])
            for layer in range(LAYERS):
                part[c, layer, row : row + 1, :] = part[c, layer, row : row + 1, :] + delta[layer : layer + 1]

    edges[0].wait()
    edges[1].wait()
    end = p // (HALF - 1)
    swap = pltpu.make_async_remote_copy(
        src_ref=az_in.at[end],
        dst_ref=az_swap,
        send_sem=edge_send.at[4],
        recv_sem=edge_recv.at[4],
        device_id=partner,
        device_id_type=MESH,
    )
    at_end = (p == 0) | (p == HALF - 1)

    @pl.when(at_end)
    def _():
        swap.start()

    loads[6].wait()
    loads[7].wait()
    products = [jnp.zeros((16, ROWS), F32) for _ in range(4)]
    for k in (0, 1, 7, 2, 6, 3, 5, 4):
        from_rad = (rad + k) % RAD
        pair = gathered.at[:, from_rad] if k else gathered.at[pl.ds(0, 1), from_rad]
        pltpu.make_async_copy(pair, pair, column_sem.at[k]).wait()
        both = (gathered[0, from_rad] + gathered[1, from_rad]) * (1.0 / NAZ)
        modes = jnp.concatenate([both[0:4], both[4:8]], axis=1)
        modes = jnp.concatenate([modes] * 4, axis=0).astype(BF16)
        at = pl.ds(pl.multiple_of(from_rad * ROWS, ROWS), ROWS)
        for n in range(4):
            products[n] += lax.dot_general(modes, kern[n // 2, n % 2, :, at], NT, preferred_element_type=F32)
    for n in range(4):
        m = n % 2
        coef[az, 2 * n : 2 * n + 2, :] = products[n][2 * m : 2 * m + 2]

    def to_plane(half, slot, targets, sent, received):
        for to in targets:
            pltpu.make_async_remote_copy(
                src_ref=coef.at[slot],
                dst_ref=coef.at[slot],
                send_sem=send_sem.at[sent],
                recv_sem=recv_sem.at[received],
                device_id=(half * HALF + to, rad),
                device_id_type=MESH,
            ).start()

    near_end = rad < RAD // 2
    roles = (
        ((z_hi == 1) & near_end, 11, 0),
        ((z_hi == 1) & jnp.logical_not(near_end), 5, 0),
        ((z_hi == 0) & near_end, 0, 11),
        ((z_hi == 0) & jnp.logical_not(near_end), 0, 5),
    )
    cross = pltpu.make_async_remote_copy(
        src_ref=coef.at[az],
        dst_ref=coef.at[az],
        send_sem=send_sem.at[2],
        recv_sem=recv_sem.at[1],
        device_id=partner,
        device_id_type=MESH,
    )
    cross.start()
    for role, direct, _ in roles:

        @pl.when(role)
        def _(targets=plane[:direct]):
            to_plane(1 - z_hi, az, targets, 5, 3)

    to_plane(z_hi, az, plane, 3, 2)

    @pl.when(at_end)
    def _():
        swap.wait()
        az_in[end] = az_swap[...]

    loads[5].wait()
    own_low, own_high = pairs_of(az_out, 0), pairs_of(az_out, 1)
    sounds = (ltab[0:1, :], ltab[1:2, :])
    used = azimuth_flux(own_high, own_low, *sounds)
    below = azimuth_flux(pairs_of(az_in, 0), own_low, *sounds)
    above = azimuth_flux(own_high, pairs_of(az_in, 1), *sounds)
    blank = jnp.zeros((2, ROWS), F32)
    weight = ltab[2:3, :]
    first = jnp.concatenate([weight * (a - b) for a, b in zip(below, used)] + [blank], axis=0)
    last = jnp.concatenate([weight * (b - a) for a, b in zip(above, used)] + [blank], axis=0)
    lane_id = lax.broadcasted_iota(jnp.int32, (ROWS, 128), 1)
    for at, lane, rim in ((0, 0, first.T), (CELLS - 128, 127, last.T)):
        for f in range(6):
            here = (f // 2, f % 2, slice(None), pl.ds(at, 128))
            delta = jnp.broadcast_to(rim[:, f : f + 1], (ROWS, 128))
            part[here] = part[here] + jnp.where(lane_id == lane, delta, 0.0)

    cross.wait_recv()
    for role, _, direct in roles:

        @pl.when(role)
        def _(targets=plane[direct:]):
            to_plane(z_hi, partner[0], targets, 4, 3)

    whole(coef, 15)(recv_sem.at[2])
    loads[8].wait()
    loads[9].wait()
    gravity = synthesis(coef, z_hi, syn, sides)
    block = 32

    @pl.loop(0, ROWS // block)
    def _(n):
        first_row = pl.multiple_of(n * block, block)
        here = pl.ds(first_row, block)
        potential, radial, azimuthal = gravity(here, rtab)
        pot[here, :] = potential
        for layer in range(LAYERS):
            rho = fluid[0, layer, pl.ds(first_row + 8, block), :]
            part[1, layer, here, :] = part[1, layer, here, :] + rho * radial
            part[2, layer, here, :] = part[2, layer, here, :] + rho * azimuthal

    whole(coef, 15)(recv_sem.at[3])
    cross.wait_send()
    for role, sent, passed_by in roles:

        @pl.when(role)
        def _(sent=sent, handed_on=15 - passed_by):
            if sent:
                whole(coef, sent)(send_sem.at[5])
            if handed_on:
                whole(coef, handed_on)(send_sem.at[4])

    for n in (0, 3):
        whole(coef, 15)(send_sem.at[n])
    whole(coef.at[:, :, pl.ds(0, 128)], 15)(send_sem.at[1])


def finish(coef, part, fluid, syn, rtab, pot, out_density, out_r, out_phi, out_pot, sides, pot_buf, mom_buf, sem):
    first = pltpu.make_async_copy(part.at[0], out_density, sem.at[0])
    first.start()
    gravity = synthesis(coef, 1 - lax.axis_index("az") // HALF, syn, sides)
    block = 64
    copies = []
    for n in range(ROWS // block):
        here = slice(n * block, (n + 1) * block)
        potential, radial, azimuthal = gravity(here, rtab)
        pot_buf[here, :] = pot[here, :] + potential
        inside = slice(8 + n * block, 8 + (n + 1) * block)
        for layer in range(LAYERS):
            rho = fluid[0, layer, inside, :]
            mom_buf[0, layer, here, :] = part[1, layer, here, :] + rho * radial
            mom_buf[1, layer, here, :] = part[2, layer, here, :] + rho * azimuthal
        rows = pl.ds(n * block, block)
        for k, (src, dst) in enumerate(
            (
                (pot_buf.at[rows, :], out_pot.at[rows, :]),
                (mom_buf.at[0, :, rows, :], out_r.at[:, rows, :]),
                (mom_buf.at[1, :, rows, :], out_phi.at[:, rows, :]),
            )
        ):
            copy = pltpu.make_async_copy(src, dst, sem.at[1 + 3 * n + k])
            copy.start()
            copies.append(copy)
    first.wait()
    for copy in copies:
        copy.wait()


def local(density, mom_r, mom_phi, potential_kernel, force_kernel):
    analysis, tables = (jnp.asarray(table) for table in mode_tables())
    rows, lanes = (jnp.asarray(table) for table in row_tables())
    operands = (density, mom_r, mom_phi, potential_kernel, force_kernel, analysis, tables, rows, lanes)
    hbm = pl.BlockSpec(memory_space=pltpu.HBM)
    vmem = pl.BlockSpec(memory_space=pltpu.VMEM)
    dma = pltpu.SemaphoreType.DMA
    shared = (
        ((AZ, 8, ROWS), F32),
        ((3, LAYERS, ROWS, CELLS), F32),
        ((3, LAYERS, ROWS + 16, CELLS), F32),
        ((2, 2, 3, 64, CELLS), BF16),
        ((ROWS, 128), F32),
        ((ROWS, CELLS), F32),
    )
    shared = pl.pallas_call(
        exchange,
        out_shape=[pltpu.VMEM(shape, dtype) for shape, dtype in shared],
        in_specs=[hbm] * 9,
        out_specs=[vmem] * 6,
        scratch_shapes=[
            pltpu.VMEM((2, 128, CELLS), BF16),
            pltpu.VMEM((2, ROWS, 192), BF16),
            pltpu.VMEM((2, 2, ROWS, NR), BF16),
            pltpu.VMEM((8, ROWS), F32),
            pltpu.VMEM((2, ROWS, CELLS), BF16),
            pltpu.VMEM((HALF, 8, ROWS), F32),
            pltpu.VMEM((15, 8, ROWS), F32),
            pltpu.VMEM((2, 8, 128), F32),
            pltpu.VMEM((2, RAD, 8, 128), F32),
            pltpu.VMEM((2, 8, ROWS), F32),
            pltpu.VMEM((2, 8, ROWS), F32),
            pltpu.VMEM((8, ROWS), F32),
            pltpu.VMEM((2, 8, CELLS), F32),
            pltpu.VMEM((2, 8, CELLS), F32),
            pltpu.VMEM((3, LAYERS, 8, CELLS), F32),
            dma((10,)),
            dma((6,)),
            dma((4,)),
            dma((RAD,)),
            dma((5,)),
            dma((5,)),
        ],
        compiler_params=pltpu.CompilerParams(
            collective_id=0, has_side_effects=True, vmem_limit_bytes=32 * 2**20
        ),
        name="exchange",
    )(*(pltpu.with_memory_space_constraint(a, pltpu.HBM) for a in operands))
    fluid_shape = jax.ShapeDtypeStruct((LAYERS, ROWS, CELLS), F32)
    return pl.pallas_call(
        finish,
        out_shape=[fluid_shape, fluid_shape, fluid_shape, jax.ShapeDtypeStruct((ROWS, CELLS), F32)],
        in_specs=[vmem] * 6,
        out_specs=[hbm] * 4,
        scratch_shapes=[
            pltpu.VMEM((2, ROWS, 192), BF16),
            pltpu.VMEM((ROWS, CELLS), F32),
            pltpu.VMEM((2, LAYERS, ROWS, CELLS), F32),
            dma((1 + 3 * 4,)),
        ],
        compiler_params=pltpu.CompilerParams(vmem_limit_bytes=32 * 2**20),
        name="finish",
    )(*shared)


def solution(mesh):
    fluid = P(None, "rad", "az")
    kernel = P("az", "rad", None)
    return jax.shard_map(
        local,
        mesh=mesh,
        in_specs=(fluid, fluid, fluid, kernel, kernel),
        out_specs=(fluid, fluid, fluid, P("rad", "az")),
        check_vma=False,
    )
```

```python
import math

import jax
import jax.numpy as jnp
import ml_dtypes
import numpy as np
from jax import lax
from jax.experimental import pallas as pl
from jax.experimental.pallas import tpu as pltpu
from jax.sharding import PartitionSpec as P

NR = 2048
NAZ = 16384
MODES = 64
AZ = 32
RAD = 8
HALF = 16
LAYERS = 2
ROWS = NR // RAD
CELLS = NAZ // AZ
STEP = 2.0 * math.pi / NAZ
ASPECT_SQ = 0.0025
MESH = pl.DeviceIdType.MESH
F32 = jnp.float32
BF16 = jnp.bfloat16
NT = (((1,), (1,)), ((), ()))
NN = (((1,), (0,)), ((), ()))


def split(table):
    high = table.astype(ml_dtypes.bfloat16)
    low = (table - high.astype(np.float64)).astype(ml_dtypes.bfloat16)
    return (high, low)


def mode_tables():
    p, h, j = np.meshgrid(np.arange(16), np.arange(2), np.arange(4), indexing="ij")
    column = 4 * (16 * h + p) + j
    mode = (column // 2).astype(np.float64)[..., None]
    odd = (column % 2).astype(bool)[..., None]
    angle = mode * ((np.arange(NAZ) + 0.5) * STEP)
    cos, sin = np.cos(angle), np.sin(angle)
    basis = np.where(odd, sin, cos)
    slope = np.where(odd, mode * cos, -mode * sin)
    analysis = np.stack(split(basis)).reshape(2, 128, AZ, CELLS).transpose(2, 0, 1, 3)
    synthesis = np.stack([split(basis), split(slope)]).transpose(0, 1, 3, 2, 4, 5)
    synthesis = synthesis.reshape(2, 2, 2, 64, AZ, CELLS).transpose(4, 2, 0, 1, 3, 5)
    return (np.ascontiguousarray(analysis), np.ascontiguousarray(synthesis))


def row_tables():
    face = np.exp(np.arange(NR + 1) * STEP)
    inner, outer = face[:-1], face[1:]
    mid = 0.5 * (inner + outer)
    area = 0.5 * (outer * outer - inner * inner)
    table = np.zeros((NR, 128), np.float32)
    columns = [
        ASPECT_SQ / outer,
        np.sqrt(ASPECT_SQ / outer),
        0.05 * STEP * outer / area,
        0.05 * STEP * inner / area,
        ASPECT_SQ / mid,
        np.sqrt(ASPECT_SQ / mid),
        0.05 / mid,
        0.1 * STEP / mid,
        0.1 * STEP * (ASPECT_SQ / mid / mid - 1.0 / (mid * mid)),
        -0.1 / mid,
        ASPECT_SQ / inner,
        np.sqrt(ASPECT_SQ / inner),
    ]
    for k, values in enumerate(columns):
        table[:, k] = values
    across = np.zeros((8, NR), np.float32)
    for k, n in enumerate((4, 5, 6)):
        across[k] = columns[n]
    return (table, across)


def face_flux(low, high, sound, sound_root, pressed):
    rho_l, mr_l, mp_l, v_l = low
    rho_h, mr_h, mp_h, v_h = high
    speed = jnp.maximum(jnp.abs(v_l), jnp.abs(v_h)) + sound_root
    a, b = v_l + speed, v_h - speed
    flux = [rho_l * a + rho_h * b, mr_l * a + mr_h * b, mp_l * a + mp_h * b]
    flux[pressed] = flux[pressed] + sound * (rho_l + rho_h)
    return flux


def reciprocal(value):
    guess = pl.reciprocal(value, approx=True)
    return guess * (2.0 - value * guess)


def whole(ref, count):
    slots = ref.at[pl.ds(0, count)]
    return lambda sem: pltpu.make_async_copy(slots, slots, sem).wait()


def radial_flux(low, high, sound, sound_root):
    return face_flux(
        (*low, low[1] * reciprocal(low[0])),
        (*high, high[1] * reciprocal(high[0])),
        sound,
        sound_root,
        1,
    )


def azimuth_flux(low, high, sound, sound_root):
    return face_flux(
        (*low, low[2] * reciprocal(low[0])),
        (*high, high[2] * reciprocal(high[0])),
        sound,
        sound_root,
        2,
    )


def pairs_of(ref, at):
    value = ref[at]
    return [value[2 * c : 2 * c + 2] for c in range(3)]


def stacked(tiles):
    value = jnp.concatenate(tiles, axis=0)
    high = value.astype(BF16).astype(F32)
    return jnp.concatenate([high, high, value - high], axis=0).T.astype(BF16)


def synthesis(coef, half, syn, sides):
    row_id = lax.broadcasted_iota(jnp.int32, (8, ROWS), 0)
    pots, forces = [], []
    for n in range(0, HALF, 2):
        a, b = coef[half * HALF + n], coef[half * HALF + n + 1]
        pots.append(jnp.where(row_id < 4, a, pltpu.roll(b, 4, 0)))
        forces.append(jnp.where(row_id < 4, pltpu.roll(a, 4, 0), b))
    sides[0] = stacked(pots)
    sides[1] = stacked(forces)

    def product(here, side, table):
        weights = syn[half, table].reshape(192, CELLS)
        return lax.dot_general(sides[side, here, :], weights, NN, preferred_element_type=F32)

    def at(here, rtab):
        radial = 0.1 * product(here, 1, 0)
        azimuthal = product(here, 0, 1) * rtab[here, 9:10]
        return product(here, 0, 0), radial, azimuthal

    return at


def exchange(
    density,
    mom_r,
    mom_phi,
    pot_kernel,
    force_kernel,
    analysis,
    tables,
    rows,
    lanes,
    coef,
    part,
    fluid,
    syn,
    rtab,
    pot,
    tab,
    sides,
    kern,
    ltab,
    chunks,
    arrived,
    halfsum,
    gathered,
    az_out,
    az_in,
    az_swap,
    rad_out,
    rad_in,
    carry,
    load_sem,
    send_sem,
    recv_sem,
    column_sem,
    edge_send,
    edge_recv,
):
    az = lax.axis_index("az")
    rad = lax.axis_index("rad")
    z_hi = az // HALF
    p = az % HALF
    y, x = p // 4, p % 4
    z, core = z_hi * 4 + rad // 2, rad % 2
    q = z_hi * RAD + rad
    partner = ((az + HALF) % AZ, rad)

    far = [(2, 2), (1, 2), (2, 1), (3, 2), (2, 3), (1, 1), (3, 3), (1, 3), (3, 1), (2, 0), (0, 2), (0, 1), (1, 0), (0, 3), (3, 0)]
    plane = [(y + dy) % 4 * 4 + (x + dx) % 4 for dy, dx in far]
    column = []
    for dz, dc in [(4, 0), (4, 1), (3, 0), (5, 0), (3, 1), (5, 1), (2, 0), (6, 0), (2, 1), (6, 1), (1, 0), (7, 0), (1, 1), (7, 1), (0, 1)]:
        there = (z + dz) % 8
        column.append((there // 4, there % 4 * 2 + (core + dc) % 2))

    barrier = pltpu.get_barrier_semaphore()
    for to in plane:
        pl.semaphore_signal(barrier, inc=1, device_id=(z_hi * HALF + to, rad), device_id_type=MESH)
    for half, to in column:
        pl.semaphore_signal(barrier, inc=1, device_id=(half * HALF + p, to), device_id_type=MESH)

    inside = pl.ds(8, ROWS)
    halves = (pl.ds(0, CELLS // 2), pl.ds(CELLS // 2, CELLS // 2))
    loads = [
        pltpu.make_async_copy(density.at[:, :, halves[0]], fluid.at[0, :, inside, halves[0]], load_sem.at[0]),
        pltpu.make_async_copy(analysis.at[az], tab, load_sem.at[1]),
        pltpu.make_async_copy(mom_r, fluid.at[1, :, inside, :], load_sem.at[2]),
        pltpu.make_async_copy(mom_phi, fluid.at[2, :, inside, :], load_sem.at[3]),
        pltpu.make_async_copy(rows.at[pl.ds(rad * ROWS, ROWS), :], rtab, load_sem.at[4]),
        pltpu.make_async_copy(lanes.at[:, pl.ds(rad * ROWS, ROWS)], ltab, load_sem.at[5]),
        pltpu.make_async_copy(pot_kernel, kern.at[0], load_sem.at[6]),
        pltpu.make_async_copy(force_kernel, kern.at[1], load_sem.at[7]),
        pltpu.make_async_copy(tables.at[az], syn.at[:, :, pl.ds(0, 2)], load_sem.at[8]),
        pltpu.make_async_copy(tables.at[az, :, :, 0], syn.at[:, :, 2], load_sem.at[9]),
    ]
    second = pltpu.make_async_copy(
        density.at[:, :, halves[1]], fluid.at[0, :, inside, halves[1]], load_sem.at[10]
    )
    for load in (loads[0], loads[1], second):
        load.start()

    share = jnp.zeros((128, ROWS), F32)
    for load, cells in zip((loads[0], second), halves):
        load.wait()
        value = fluid[0, 0, inside, cells] + fluid[0, 1, inside, cells]
        high = value.astype(BF16)
        low = (value - high.astype(F32)).astype(BF16)
        if load is second:
            for later in loads[2:]:
                later.start()
        else:
            loads[1].wait()
        share += lax.dot_general(tab[0, :, cells], high, NT, preferred_element_type=F32)
        share += lax.dot_general(tab[0, :, cells], low, NT, preferred_element_type=F32)
        share += lax.dot_general(tab[1, :, cells], high, NT, preferred_element_type=F32)
    chunks[...] = share.reshape(HALF, 8, ROWS)

    pl.semaphore_wait(barrier, len(plane) + len(column))

    for k, to in enumerate(plane):
        pltpu.make_async_remote_copy(
            src_ref=chunks.at[to],
            dst_ref=arrived.at[k],
            send_sem=send_sem.at[0],
            recv_sem=recv_sem.at[0],
            device_id=(z_hi * HALF + to, rad),
            device_id_type=MESH,
        ).start()

    loads[2].wait()
    loads[3].wait()
    row_id = lax.broadcasted_iota(jnp.int32, (8, 256), 0)
    lane_id = lax.broadcasted_iota(jnp.int32, (8, 256), 1)
    for side, (at, lane) in enumerate(((0, 0), (CELLS - 128, 127))):
        total = jnp.zeros((8, ROWS), F32)
        for c in range(3):
            both = jnp.concatenate([fluid[c, n, inside, at : at + 128] for n in range(2)], axis=1)
            pick = jnp.where(lane_id == lane + 128 * (row_id - 2 * c), 1.0, 0.0)
            pick = jnp.where((row_id == 2 * c) | (row_id == 2 * c + 1), pick, 0.0).astype(BF16)
            high = both.astype(BF16)
            low = (both - high.astype(F32)).astype(BF16)
            total += lax.dot_general(pick, high, NT, preferred_element_type=F32)
            total += lax.dot_general(pick, low, NT, preferred_element_type=F32)
        az_out[side] = total
    rad_out[...] = jnp.zeros_like(rad_out)
    for f in range(6):
        rad_out[0, f : f + 1, :] = fluid[f // 2, f % 2, 8:9, :]
        rad_out[1, f : f + 1, :] = fluid[f // 2, f % 2, 8 + ROWS - 1 : 8 + ROWS, :]
    edges = []
    for n, (src, dst, device) in enumerate(
        (
            (az_out.at[0], az_in.at[1], (z_hi * HALF + (p + HALF - 1) % HALF, rad)),
            (az_out.at[1], az_in.at[0], (z_hi * HALF + (p + 1) % HALF, rad)),
            (rad_out.at[0], rad_in.at[1], (az, (rad + RAD - 1) % RAD)),
            (rad_out.at[1], rad_in.at[0], (az, (rad + 1) % RAD)),
        )
    ):
        copy = pltpu.make_async_remote_copy(
            src_ref=src,
            dst_ref=dst,
            send_sem=edge_send.at[n],
            recv_sem=edge_recv.at[n],
            device_id=device,
            device_id_type=MESH,
        )
        copy.start()
        edges.append(copy)

    loads[4].wait()
    for c in range(3):
        for layer in range(LAYERS):
            fluid[c, layer, 0:8, :] = jnp.broadcast_to(fluid[c, layer, 8:9, :], (8, CELLS))
            fluid[c, layer, 8 + ROWS : 16 + ROWS, :] = jnp.broadcast_to(
                fluid[c, layer, 7 + ROWS : 8 + ROWS, :], (8, CELLS)
            )
    for layer in range(LAYERS):
        edge = [fluid[c, layer, 0:8, :] for c in range(3)]
        flux = radial_flux(edge, edge, rtab[0:1, 10:11], rtab[0:1, 11:12])
        for c in range(3):
            carry[c, layer] = flux[c]

    size = 32

    def update(block):
        at = pl.multiple_of(block * size, size)
        here = pl.ds(at, size)

        def factor(k):
            return jnp.broadcast_to(rtab[here, k : k + 1], (size, CELLS))

        for layer in range(LAYERS):
            state = [fluid[c, layer, pl.ds(at + 8, size + 8), :] for c in range(3)]
            inv = reciprocal(state[0])
            state.append(state[1] * inv)
            low = [value[:size] for value in state]
            high = [pltpu.roll(value, size + 7, 0)[:size] for value in state]
            flux = face_flux(low, high, factor(0), factor(1), 1)
            rho, mr, mp = low[:3]
            vp = mp * inv[:size]
            cells = (rho, mr, mp, vp)
            left = [pltpu.roll(value, 1, 1) for value in cells]
            side = face_flux(left, cells, factor(4), factor(5), 2)
            new = []
            for c in range(3):
                below = pltpu.roll(jnp.concatenate([carry[c, layer], flux[c]], axis=0), 1, 0)[8:]
                above = pltpu.roll(side[c], CELLS - 1, 1)
                carry[c, layer] = flux[c][size - 8 :]
                new.append(
                    low[c]
                    - (factor(2) * flux[c] - factor(3) * below + factor(6) * (above - side[c]))
                )
            turn = factor(7) * vp
            new[1] = new[1] + (turn * mp + factor(8) * rho)
            new[2] = new[2] - turn * mr
            for c in range(3):
                part[c, layer, here, :] = new[c]

    early = 4
    pl.loop(0, early)(update)

    whole(arrived, 15)(recv_sem.at[0])
    total = chunks[p]
    for k in range(15):
        total = total + arrived[k]
    for h in range(2):
        halfsum[h, 0:4, :] = total[4 * h : 4 * h + 4, 0:128]
        halfsum[h, 4:8, :] = total[4 * h : 4 * h + 4, 128:256]
    gathered[z_hi, rad] = halfsum[z_hi]
    for half, to in column:
        pltpu.make_async_remote_copy(
            src_ref=halfsum.at[half],
            dst_ref=gathered.at[z_hi, rad],
            send_sem=send_sem.at[1],
            recv_sem=column_sem.at[(rad - to + RAD) % RAD],
            device_id=(half * HALF + p, to),
            device_id_type=MESH,
        ).start()

    pl.loop(early, ROWS // size)(update)

    edges[2].wait()
    edges[3].wait()
    for side, (outermost, sign, weight, sound) in enumerate(
        ((rad == 0, 1.0, rtab[0:1, 3:4], 10), (rad == RAD - 1, -1.0, rtab[ROWS - 1 : ROWS, 2:3], 0))
    ):
        row = 0 if side == 0 else ROWS - 1
        sounds = (rtab[row : row + 1, sound : sound + 1], rtab[row : row + 1, sound + 1 : sound + 2])
        own = pairs_of(rad_out, side)
        beyond = [jnp.where(outermost, a, b) for a, b in zip(own, pairs_of(rad_in, side))]
        used = radial_flux(own, own, *sounds)
        right = radial_flux(beyond, own, *sounds) if side == 0 else radial_flux(own, beyond, *sounds)
        for c in range(3):
            delta = (sign * weight) * (right[c] - used[c])
            for layer in range(LAYERS):
                part[c, layer, row : row + 1, :] = part[c, layer, row : row + 1, :] + delta[layer : layer + 1]

    edges[0].wait()
    edges[1].wait()
    end = p // (HALF - 1)
    swap = pltpu.make_async_remote_copy(
        src_ref=az_in.at[end],
        dst_ref=az_swap,
        send_sem=edge_send.at[4],
        recv_sem=edge_recv.at[4],
        device_id=partner,
        device_id_type=MESH,
    )
    at_end = (p == 0) | (p == HALF - 1)

    @pl.when(at_end)
    def _():
        swap.start()

    loads[6].wait()
    loads[7].wait()
    products = [jnp.zeros((16, ROWS), F32) for _ in range(4)]
    for k in (0, 1, 7, 2, 6, 3, 5, 4):
        from_rad = (rad + k) % RAD
        pair = gathered.at[:, from_rad] if k else gathered.at[pl.ds(0, 1), from_rad]
        pltpu.make_async_copy(pair, pair, column_sem.at[k]).wait()
        both = (gathered[0, from_rad] + gathered[1, from_rad]) * (1.0 / NAZ)
        modes = jnp.concatenate([both[0:4], both[4:8]], axis=1)
        modes = jnp.concatenate([modes] * 4, axis=0).astype(BF16)
        at = pl.ds(pl.multiple_of(from_rad * ROWS, ROWS), ROWS)
        for n in range(4):
            products[n] += lax.dot_general(modes, kern[n // 2, n % 2, :, at], NT, preferred_element_type=F32)
    for n in range(4):
        m = n % 2
        coef[az, 2 * n : 2 * n + 2, :] = products[n][2 * m : 2 * m + 2]

    def to_plane(half, slot, targets, sent, received):
        for to in targets:
            pltpu.make_async_remote_copy(
                src_ref=coef.at[slot],
                dst_ref=coef.at[slot],
                send_sem=send_sem.at[sent],
                recv_sem=recv_sem.at[received],
                device_id=(half * HALF + to, rad),
                device_id_type=MESH,
            ).start()

    near_end = rad < RAD // 2
    roles = (
        ((z_hi == 1) & near_end, 11, 0),
        ((z_hi == 1) & jnp.logical_not(near_end), 5, 0),
        ((z_hi == 0) & near_end, 0, 11),
        ((z_hi == 0) & jnp.logical_not(near_end), 0, 5),
    )
    cross = pltpu.make_async_remote_copy(
        src_ref=coef.at[az],
        dst_ref=coef.at[az],
        send_sem=send_sem.at[2],
        recv_sem=recv_sem.at[1],
        device_id=partner,
        device_id_type=MESH,
    )
    cross.start()
    for role, direct, _ in roles:

        @pl.when(role)
        def _(targets=plane[:direct]):
            to_plane(1 - z_hi, az, targets, 5, 3)

    to_plane(z_hi, az, plane, 3, 2)

    @pl.when(at_end)
    def _():
        swap.wait()
        az_in[end] = az_swap[...]

    loads[5].wait()
    own_low, own_high = pairs_of(az_out, 0), pairs_of(az_out, 1)
    sounds = (ltab[0:1, :], ltab[1:2, :])
    used = azimuth_flux(own_high, own_low, *sounds)
    below = azimuth_flux(pairs_of(az_in, 0), own_low, *sounds)
    above = azimuth_flux(own_high, pairs_of(az_in, 1), *sounds)
    blank = jnp.zeros((2, ROWS), F32)
    weight = ltab[2:3, :]
    first = jnp.concatenate([weight * (a - b) for a, b in zip(below, used)] + [blank], axis=0)
    last = jnp.concatenate([weight * (b - a) for a, b in zip(above, used)] + [blank], axis=0)
    lane_id = lax.broadcasted_iota(jnp.int32, (ROWS, 128), 1)
    for at, lane, rim in ((0, 0, first.T), (CELLS - 128, 127, last.T)):
        for f in range(6):
            here = (f // 2, f % 2, slice(None), pl.ds(at, 128))
            delta = jnp.broadcast_to(rim[:, f : f + 1], (ROWS, 128))
            part[here] = part[here] + jnp.where(lane_id == lane, delta, 0.0)

    cross.wait_recv()
    for role, _, direct in roles:

        @pl.when(role)
        def _(targets=plane[direct:]):
            to_plane(z_hi, partner[0], targets, 4, 3)

    whole(coef, 15)(recv_sem.at[2])
    loads[8].wait()
    loads[9].wait()
    gravity = synthesis(coef, z_hi, syn, sides)
    block = 32

    @pl.loop(0, ROWS // block)
    def _(n):
        first_row = pl.multiple_of(n * block, block)
        here = pl.ds(first_row, block)
        potential, radial, azimuthal = gravity(here, rtab)
        pot[here, :] = potential
        for layer in range(LAYERS):
            rho = fluid[0, layer, pl.ds(first_row + 8, block), :]
            part[1, layer, here, :] = part[1, layer, here, :] + rho * radial
            part[2, layer, here, :] = part[2, layer, here, :] + rho * azimuthal

    whole(coef, 15)(recv_sem.at[3])
    cross.wait_send()
    for role, sent, passed_by in roles:

        @pl.when(role)
        def _(sent=sent, handed_on=15 - passed_by):
            if sent:
                whole(coef, sent)(send_sem.at[5])
            if handed_on:
                whole(coef, handed_on)(send_sem.at[4])

    for n in (0, 3):
        whole(coef, 15)(send_sem.at[n])
    whole(coef.at[:, :, pl.ds(0, 128)], 15)(send_sem.at[1])


def finish(coef, part, fluid, syn, rtab, pot, out_density, out_r, out_phi, out_pot, sides, pot_buf, mom_buf, sem):
    first = pltpu.make_async_copy(part.at[0], out_density, sem.at[0])
    first.start()
    gravity = synthesis(coef, 1 - lax.axis_index("az") // HALF, syn, sides)
    block = 64
    copies = []
    for n in range(ROWS // block):
        here = slice(n * block, (n + 1) * block)
        potential, radial, azimuthal = gravity(here, rtab)
        pot_buf[here, :] = pot[here, :] + potential
        inside = slice(8 + n * block, 8 + (n + 1) * block)
        for layer in range(LAYERS):
            rho = fluid[0, layer, inside, :]
            mom_buf[0, layer, here, :] = part[1, layer, here, :] + rho * radial
            mom_buf[1, layer, here, :] = part[2, layer, here, :] + rho * azimuthal
        rows = pl.ds(n * block, block)
        for k, (src, dst) in enumerate(
            (
                (pot_buf.at[rows, :], out_pot.at[rows, :]),
                (mom_buf.at[0, :, rows, :], out_r.at[:, rows, :]),
                (mom_buf.at[1, :, rows, :], out_phi.at[:, rows, :]),
            )
        ):
            copy = pltpu.make_async_copy(src, dst, sem.at[1 + 3 * n + k])
            copy.start()
            copies.append(copy)
    first.wait()
    for copy in copies:
        copy.wait()


def local(density, mom_r, mom_phi, potential_kernel, force_kernel):
    analysis, tables = (jnp.asarray(table) for table in mode_tables())
    rows, lanes = (jnp.asarray(table) for table in row_tables())
    operands = (density, mom_r, mom_phi, potential_kernel, force_kernel, analysis, tables, rows, lanes)
    hbm = pl.BlockSpec(memory_space=pltpu.HBM)
    vmem = pl.BlockSpec(memory_space=pltpu.VMEM)
    dma = pltpu.SemaphoreType.DMA
    shared = (
        ((AZ, 8, ROWS), F32),
        ((3, LAYERS, ROWS, CELLS), F32),
        ((3, LAYERS, ROWS + 16, CELLS), F32),
        ((2, 2, 3, 64, CELLS), BF16),
        ((ROWS, 128), F32),
        ((ROWS, CELLS), F32),
    )
    shared = pl.pallas_call(
        exchange,
        out_shape=[pltpu.VMEM(shape, dtype) for shape, dtype in shared],
        in_specs=[hbm] * 9,
        out_specs=[vmem] * 6,
        scratch_shapes=[
            pltpu.VMEM((2, 128, CELLS), BF16),
            pltpu.VMEM((2, ROWS, 192), BF16),
            pltpu.VMEM((2, 2, ROWS, NR), BF16),
            pltpu.VMEM((8, ROWS), F32),
            pltpu.VMEM((HALF, 8, ROWS), F32),
            pltpu.VMEM((15, 8, ROWS), F32),
            pltpu.VMEM((2, 8, 128), F32),
            pltpu.VMEM((2, RAD, 8, 128), F32),
            pltpu.VMEM((2, 8, ROWS), F32),
            pltpu.VMEM((2, 8, ROWS), F32),
            pltpu.VMEM((8, ROWS), F32),
            pltpu.VMEM((2, 8, CELLS), F32),
            pltpu.VMEM((2, 8, CELLS), F32),
            pltpu.VMEM((3, LAYERS, 8, CELLS), F32),
            dma((11,)),
            dma((6,)),
            dma((4,)),
            dma((RAD,)),
            dma((5,)),
            dma((5,)),
        ],
        compiler_params=pltpu.CompilerParams(
            collective_id=0, has_side_effects=True, vmem_limit_bytes=32 * 2**20
        ),
        name="exchange",
    )(*(pltpu.with_memory_space_constraint(a, pltpu.HBM) for a in operands))
    fluid_shape = jax.ShapeDtypeStruct((LAYERS, ROWS, CELLS), F32)
    return pl.pallas_call(
        finish,
        out_shape=[fluid_shape, fluid_shape, fluid_shape, jax.ShapeDtypeStruct((ROWS, CELLS), F32)],
        in_specs=[vmem] * 6,
        out_specs=[hbm] * 4,
        scratch_shapes=[
            pltpu.VMEM((2, ROWS, 192), BF16),
            pltpu.VMEM((ROWS, CELLS), F32),
            pltpu.VMEM((2, LAYERS, ROWS, CELLS), F32),
            dma((1 + 3 * 4,)),
        ],
        compiler_params=pltpu.CompilerParams(vmem_limit_bytes=32 * 2**20),
        name="finish",
    )(*shared)


def solution(mesh):
    fluid = P(None, "rad", "az")
    kernel = P("az", "rad", None)
    return jax.shard_map(
        local,
        mesh=mesh,
        in_specs=(fluid, fluid, fluid, kernel, kernel),
        out_specs=(fluid, fluid, fluid, P("rad", "az")),
        check_vma=False,
    )
```
